32 devices in a mesh: groups: 1, node: 32 (over z, y, x, core).
Axes of the slice: x: 2, y: 2, z: 4, core: 2. Of those that a mesh axis runs over, the one named last changes fastest.
Arguments:
- hidden_in: bfloat16 [128, 4096], P(('groups', 'node')), may hold values from -6 to 6
- queries: bfloat16 [128, 8192], P(('groups', 'node')), may hold values from -90 to 90
- new_kv: bfloat16 [128, 2, 512], P(('groups', 'node')), may hold values from -5 to 5
- kv_cache: bfloat16 [128, 2, 256, 512], P(('groups', 'node')), may hold values from -5 to 5
- lengths: int32 [128], P(('groups', 'node')), may hold values from 1 to 256, as said below
- w_out: bfloat16 [8192, 4096], P('node'), may hold values from -0.25 to 0.25
- w_gate: bfloat16 [32, 4096, 384], P('node'), may hold values from -0.09375 to 0.09375
- w_up: bfloat16 [32, 4096, 384], P('node'), may hold values from -0.09375 to 0.09375
- w_down: bfloat16 [32, 384, 4096], P('node'), may hold values from -0.21875 to 0.21875
- mlp_gain: float32 [4096], replicated, may hold values from 0.1 to 1.9
- expert_ids: int32 [128, 8], P(('groups', 'node')), may hold values from 0 to 15, all different within a row; in each aligned block of 4 rows (0 to 3, 4 to 7, ...) at most 2 rows name the same one
- route_weight: float32 [128, 8], P(('groups', 'node')), may hold values from 0.05 to 0.4
Outputs:
- attn_out: bfloat16 [128, 4096], P(('groups', 'node'))
- layer_out: bfloat16 [128, 4096], P(('groups', 'node'))
The draws below stay inside these ranges and needn't reach their ends.
Inputs may be any that keep to these rules, and one draw needn't show every extreme that they name: `expert_ids`: each row names 8 different experts; within the rows of one device no expert is named more than 2 times, and exactly 2 times in some devices' rows. `lengths`: the largest value 256 is reached in every draw; positions at or past a row's length hold stale entries.
All inputs are finite; a program needn't handle non-finite values.
Results may differ from the reference program's by a relative error of at most 0.008.
Values may be sent and summed in bfloat16 or wider, within the bound.
No kernel may reach another device: no remote copies, remote signals or barrier semaphores. Data moves between devices by JAX's collectives and lax.ppermute only.
A program may use at most 64 MiB of HBM per device.

```python
import math
import jax
import jax.numpy as jnp
import numpy as np
from jax import lax

D = 4096
Q_HEADS = 64
KV_HEADS = 4
HEAD = 128
FF = 768
TOP = 8
ROWS_DEV = 4
CACHE = 256
EXPERTS = 16
ROWS = 128
CAP = 2
N_NODE = 32


def shared_cache(key):
    base_cache = jax.random.normal(key, (ROWS, 2, CACHE, KV_HEADS * HEAD), jnp.float32)
    return jnp.clip(base_cache, -5.0, 5.0)


def draw_kv_cache(key, part):
    base_cache = shared_cache(key)
    return base_cache.astype(jnp.bfloat16)


def draw_queries(key, part):
    key = jax.random.fold_in(key, 7)
    drawn_draw = jnp.clip(jax.random.normal(key, (ROWS, Q_HEADS * HEAD), jnp.float32), -5.0, 5.0)
    return drawn_draw.astype(jnp.bfloat16)


def draw_new_kv(key, part):
    key = jax.random.fold_in(key, 9)
    drawn_draw = jnp.clip(jax.random.normal(key, (ROWS, 2, KV_HEADS * HEAD), jnp.float32), -5.0, 5.0)
    return drawn_draw.astype(jnp.bfloat16)


def draw_lengths(key, part):
    key = jax.random.fold_in(key, 21)
    spread = jax.random.randint(jax.random.fold_in(key, 1), (ROWS,), 0, CACHE)
    factor = jax.random.randint(jax.random.fold_in(key, 2), (ROWS // ROWS_DEV, 1), 1, 5)
    factor = jnp.broadcast_to(factor, (ROWS // ROWS_DEV, ROWS_DEV)).reshape(ROWS)
    lengths = 1 + spread * factor // 4
    longest = jax.random.randint(jax.random.fold_in(key, 3), (), 0, ROWS)
    return jnp.where(jnp.arange(ROWS) == longest, CACHE, lengths).astype(jnp.int32)


def shard_levels(rng, extent, split, low, largest):
    level = 1.0
    for dim, parts in split:
        draws = jax.random.uniform(jax.random.fold_in(jax.random.fold_in(rng, 6), dim), (parts,), jnp.float32, low / len(split), largest / len(split))
        level = level * jnp.repeat(jnp.exp(draws), extent[dim] // parts).reshape((-1,) + (1,) * (len(extent) - 1 - dim))
    return level


def routed_block(key, own, number, rows, amount, top, reach, skew):
    order = jax.random.permutation(key, amount)
    crowded, usual = load_shares(amount, rows * top, reach, skew, True), load_shares(amount, rows * top, reach, skew, False)
    places = jnp.arange(amount)

    def named(sizes, turn):
        used = int((sizes > 0).sum())
        fixed = max(1, used // 4)
        passed = fixed + (places - fixed + turn * (used - fixed)) % max(1, amount - fixed)
        return jnp.zeros((amount,), jnp.int32).at[order[jnp.where(places < fixed, places, passed)]].set(jnp.asarray(sizes, jnp.int32))

    sizes = jnp.where(number % 4 == 0, named(crowded, number // 4), named(usual, number - number // 4 - 1))
    mixed = jax.random.permutation(jax.random.fold_in(own, 3), amount)
    donor, taker = mixed[0:amount // 2 * 2:2], mixed[1:amount // 2 * 2:2]
    margin = jnp.minimum(sizes[donor] - 1, reach - sizes[taker]) // 2
    margin = jnp.where((donor == order[0]) | (taker == order[0]) | (sizes[taker] == 0), 0, jnp.maximum(margin, 0))
    passed = jax.random.randint(jax.random.fold_in(own, 4), (amount // 2,), 0, 1 << 20) % (margin + 1)
    sizes = sizes.at[donor].add(-passed).at[taker].add(passed)
    labels = jnp.searchsorted(jnp.cumsum(sizes), jnp.arange(rows * top), side="right").astype(jnp.int32)
    table = labels.reshape(top, rows).T
    table = table[jax.random.permutation(jax.random.fold_in(own, 1), rows)]
    turn = jax.random.randint(jax.random.fold_in(own, 2), (rows, 1), 0, top)
    return jnp.take_along_axis(table, (jnp.arange(top)[None, :] + turn) % top, axis=1)


def load_shares(count, total, reach, skew, full):
    weights = [(1 << 20) // math.isqrt(rank ** skew) + 1 for rank in range(1, count + 1)]
    largest = reach if full else min(reach, max(-(-total // count), total * weights[0] // sum(weights)))
    least = 1 if total - largest >= count - 1 else 0
    given, rest = [largest] + [least] * (count - 1), total - largest - least * (count - 1)
    while rest > 0:
        movable = [i for i in range(1, count) if given[i] < largest] or [i for i in range(1, count) if given[i] < reach]
        mass, left = sum([weights[i] for i in movable]), rest
        for i in movable:
            more = min(reach - given[i], max(1, left * weights[i] // mass), rest)
            given[i] = given[i] + more
            rest = rest - more
    return np.array(given)


def normal_values(stream_key, shape, width, bound, split=(), kind=jnp.bfloat16):
    array = jax.random.normal(stream_key, shape, jnp.float32) * width
    if len(split) > 0:
        array = shard_levels(stream_key, shape, split, -0.22, 0.18) * array
    return jnp.clip(array, min=-bound, max=bound).astype(kind)


def setup_inputs(seed: int = 0, part: int = 0) -> dict:
    key_list = jax.random.split(jax.random.key(seed), 13)
    part_splits = jax.random.split(jax.random.fold_in(key_list[12], part), 13)
    hidden_in = normal_values(part_splits[0], (ROWS, D), 1.0, 6.0, ((0, 32),))
    queries = draw_queries(jax.random.fold_in(jax.random.fold_in(key_list[12], part), 71), part)
    new_kv = draw_new_kv(jax.random.fold_in(jax.random.fold_in(key_list[12], part), 71), part)
    kv_cache = draw_kv_cache(jax.random.fold_in(jax.random.fold_in(key_list[12], part), 71), part)
    lengths = draw_lengths(jax.random.fold_in(jax.random.fold_in(key_list[12], part), 71), part)
    w_out = normal_values(key_list[5], (Q_HEADS * HEAD, D), (Q_HEADS * HEAD // 16) ** -0.5, 0.25, ((0, 32),))
    w_gate = normal_values(key_list[6], (2 * EXPERTS, D, FF // 2), D ** -0.5, 0.09375, ((0, 32),))
    w_up = normal_values(key_list[7], (2 * EXPERTS, D, FF // 2), D ** -0.5, 0.09375, ((0, 32),))
    w_down = normal_values(key_list[8], (2 * EXPERTS, FF // 2, D), FF ** -0.5, 0.21875, ((0, 32),))
    mlp_gain = jnp.clip(1.0 + 0.18 * jax.random.normal(key_list[9], (D,), jnp.float32), 0.1, 1.9)
    expert_ids_keys = jax.random.split(jax.random.fold_in(part_splits[10], 1), ROWS // ROWS_DEV)
    expert_ids_turns = jax.random.permutation(jax.random.fold_in(part_splits[10], 3), ROWS // ROWS_DEV)
    expert_ids = jax.vmap(lambda own, number: routed_block(jax.random.fold_in(part_splits[10], 2), own, number, ROWS_DEV, EXPERTS, TOP, CAP, 2))(expert_ids_keys, expert_ids_turns).reshape((ROWS, TOP))
    route_weight = jnp.clip(0.05 + 0.35 * jax.random.uniform(part_splits[11], (ROWS, TOP), jnp.float32) ** shard_levels(part_splits[11], (ROWS, TOP), ((0, 32),), -0.2, 0.2), 0.05, 0.4)
    return dict(hidden_in=hidden_in, queries=queries, new_kv=new_kv, kv_cache=kv_cache, lengths=lengths, w_out=w_out, w_gate=w_gate, w_up=w_up, w_down=w_down, mlp_gain=mlp_gain, expert_ids=expert_ids, route_weight=route_weight)


def softmax_context(queries, new_kv, kv_cache, lengths):
    row_count = queries.shape[0]
    group_size = Q_HEADS // KV_HEADS
    query_grid = queries.reshape(row_count, KV_HEADS, group_size, HEAD).astype(jnp.float32)
    cache_keys = kv_cache[:, 0].reshape(row_count, CACHE, KV_HEADS, HEAD).astype(jnp.float32)
    cache_values = kv_cache[:, 1].reshape(row_count, CACHE, KV_HEADS, HEAD).astype(jnp.float32)
    fresh_key = new_kv[:, 0].reshape(row_count, KV_HEADS, HEAD).astype(jnp.float32)
    fresh_value = new_kv[:, 1].reshape(row_count, KV_HEADS, HEAD).astype(jnp.float32)
    score_scale = 1.0 / math.sqrt(HEAD)
    old_scores = jnp.einsum('rkgd,rlkd->rkgl', query_grid, cache_keys) * score_scale
    new_scores = jnp.einsum('rkgd,rkd->rkg', query_grid, fresh_key) * score_scale
    positions = jnp.arange(CACHE, dtype=jnp.int32)[None, :]
    valid_mask = (positions < lengths[:, None])[:, None, None, :]
    old_scores = jnp.where(valid_mask, old_scores, -jnp.inf)
    row_max = jnp.maximum(lax.optimization_barrier(jnp.max(old_scores, axis=-1)), new_scores)
    old_exp = jnp.exp(old_scores - row_max[..., None])
    new_exp = jnp.exp(new_scores - row_max)
    denom_sum = lax.optimization_barrier(jnp.sum(old_exp, axis=-1)) + new_exp
    old_probs = (old_exp / denom_sum[..., None]).astype(jnp.bfloat16).astype(jnp.float32)
    new_probs = (new_exp / denom_sum).astype(jnp.bfloat16).astype(jnp.float32)
    context = jnp.einsum('rkgl,rlkd->rkgd', old_probs, cache_values)
    context = context + new_probs[..., None] * fresh_value[:, :, None, :]
    return context.reshape(row_count, Q_HEADS * HEAD).astype(jnp.bfloat16)

def reference(hidden_in, queries, new_kv, kv_cache, lengths, w_out, w_gate, w_up, w_down, mlp_gain, expert_ids, route_weight):
    row_count = hidden_in.shape[0]
    context = softmax_context(queries, new_kv, kv_cache, lengths)
    attn_out = jnp.dot(context, w_out, preferred_element_type=jnp.float32).astype(jnp.bfloat16)
    mixed_state = hidden_in.astype(jnp.float32) + attn_out.astype(jnp.float32)
    mean_square = lax.optimization_barrier(jnp.mean(mixed_state * mixed_state, axis=-1, keepdims=True))
    normed = (mixed_state * lax.rsqrt(mean_square + 1e-06) * mlp_gain[None, :]).astype(jnp.bfloat16)

    def one_expert(expert):
        routed = jnp.any(expert_ids == expert, axis=1)
        slot_index = jnp.nonzero(routed, size=N_NODE * CAP, fill_value=row_count)[0].astype(jnp.int32)
        picked_rows = normed[jnp.minimum(slot_index, row_count - 1)]
        partials = []
        for half_index in range(2):
            slab = 2 * expert + half_index
            gate_val = jnp.dot(picked_rows, w_gate[slab], preferred_element_type=jnp.float32)
            up_val = jnp.dot(picked_rows, w_up[slab], preferred_element_type=jnp.float32)
            activation = (jax.nn.silu(gate_val) * up_val).astype(jnp.bfloat16)
            partials.append(jnp.dot(activation, w_down[slab], preferred_element_type=jnp.float32).astype(jnp.bfloat16))
        combined = (partials[0].astype(jnp.float32) + partials[1].astype(jnp.float32)).astype(jnp.bfloat16)
        placed = jnp.zeros((row_count, D), jnp.bfloat16)
        return placed.at[slot_index].set(combined, mode='drop')
    expert_out = lax.map(one_expert, jnp.arange(EXPERTS, dtype=jnp.int32))
    row_index = jnp.arange(row_count, dtype=jnp.int32)[:, None]
    chosen = expert_out[expert_ids, row_index].astype(jnp.float32)
    moe_sum = lax.optimization_barrier(jnp.sum(route_weight[..., None] * chosen, axis=1))
    layer_out = (mixed_state + moe_sum).astype(jnp.bfloat16)
    return (attn_out, layer_out)
```

```python
import functools
import math

import jax
import jax.numpy as jnp
from jax import lax
from jax.experimental import pallas as pl
from jax.experimental.pallas import tpu as pltpu
from jax.sharding import PartitionSpec as P

HEAD = 128
LANE = 128
F32 = jnp.float32
BF16 = jnp.bfloat16


def vmem_spec():
    return pl.BlockSpec(memory_space=pltpu.VMEM)


def smem_spec():
    return pl.BlockSpec(memory_space=pltpu.SMEM)


def attention_kernel(
    cap, q_ref, new_ref, kv_ref, len_ref, ids_ref, out_ref, slot_ref, place_ref, q32, ctx, count
):
    row = pl.program_id(0)
    rows, heads, _ = ctx.shape
    experts = slot_ref.shape[0] // cap
    cache_len = kv_ref.shape[2]
    kv_heads = kv_ref.shape[3] // HEAD
    group = heads // kv_heads

    @pl.when(row == 0)
    def _():
        for h in range(heads):
            q32[pl.ds(h, rows, stride=heads), :] = q_ref[:, h * HEAD : (h + 1) * HEAD].astype(F32)
        for e in range(experts):
            count[e] = 0
        for e in range(experts * cap):
            slot_ref[e] = 0

    for k in range(ids_ref.shape[1]):
        expert = ids_ref[row, k]
        slot = expert * cap + count[expert]
        count[expert] = count[expert] + 1
        slot_ref[slot] = row
        place_ref[row, k] = slot

    length = len_ref[row]
    scale = 1.0 / math.sqrt(HEAD)
    valid = lax.broadcasted_iota(jnp.int32, (group, cache_len), 1) < length
    for g in range(kv_heads):
        cols = slice(g * HEAD, (g + 1) * HEAD)
        query = q32[pl.ds(pl.multiple_of(row * heads, heads) + g * group, group), :]
        old = lax.dot_general(
            query.astype(BF16),
            kv_ref[0, 0, :, cols],
            (((1,), (1,)), ((), ())),
            preferred_element_type=F32,
        )
        old = jnp.where(valid, old * scale, -jnp.inf)
        fresh_key = new_ref[0, 0:1, cols].astype(F32)
        fresh_value = new_ref[0, 1:2, cols].astype(F32)
        new = jnp.sum(query * fresh_key, axis=1, keepdims=True) * scale
        top = jnp.maximum(jnp.max(old, axis=1, keepdims=True), new)
        old = jnp.exp(old - top)
        new = jnp.exp(new - top)
        denom = jnp.sum(old, axis=1, keepdims=True) + new
        probs = (old / denom).astype(BF16)
        new = (new / denom).astype(BF16).astype(F32)
        value = jnp.dot(probs, kv_ref[0, 1, :, cols], preferred_element_type=F32)
        ctx[row, g * group : (g + 1) * group, :] = value + new * fresh_value

    @pl.when(row == rows - 1)
    def _():
        chips = out_ref.shape[0] // 2
        each = heads // chips
        for i in range(chips):
            block = jnp.concatenate(
                [ctx[r, i * each : (i + 1) * each, :] for r in range(rows)], axis=0
            ).astype(BF16)
            out_ref[2 * i] = block
            out_ref[2 * i + 1] = block


def attention(queries, new_kv, kv_cache, lengths, expert_ids, devices, cap):
    rows = queries.shape[0]
    heads = queries.shape[1] // HEAD
    each = heads // (devices // 2)
    experts = devices // 2
    return pl.pallas_call(
        functools.partial(attention_kernel, cap),
        grid=(rows,),
        in_specs=[
            vmem_spec(),
            pl.BlockSpec((1,) + new_kv.shape[1:], lambda i: (i, 0, 0)),
            pl.BlockSpec((1,) + kv_cache.shape[1:], lambda i: (i, 0, 0, 0)),
            smem_spec(),
            smem_spec(),
        ],
        out_specs=[
            pl.BlockSpec((devices, rows * each, LANE), lambda i: (0, 0, 0)),
            smem_spec(),
            smem_spec(),
        ],
        out_shape=[
            jax.ShapeDtypeStruct((devices, rows * each, LANE), BF16),
            jax.ShapeDtypeStruct((experts * cap,), jnp.int32),
            jax.ShapeDtypeStruct(expert_ids.shape, jnp.int32),
        ],
        scratch_shapes=[
            pltpu.VMEM((rows * heads, LANE), F32),
            pltpu.VMEM((rows, heads, LANE), F32),
            pltpu.SMEM((experts,), jnp.int32),
        ],
        compiler_params=pltpu.CompilerParams(vmem_limit_bytes=12 << 20),
    )(queries, new_kv, kv_cache, lengths, expert_ids)


def project_kernel(core_ref, ctx_ref, own_ref, peer_ref, out_ref, x32, o32):
    devices, per, _ = ctx_ref.shape
    x32[...] = ctx_ref[...].reshape(devices * per, LANE).astype(F32)
    core = core_ref[0]
    held = own_ref.shape[0] // LANE
    each = 2 * held
    sums = o32.shape[0] * LANE // own_ref.shape[1]

    def part(first, w_ref):
        left = jnp.concatenate(
            [x32[pl.ds(first + j, sums, stride=each), :].astype(BF16) for j in range(held)],
            axis=1,
        )
        return jnp.dot(left, w_ref[...], preferred_element_type=F32)

    total = part(core * held, own_ref) + part((1 - core) * held, peer_ref)
    chunks = own_ref.shape[1] // LANE
    for t in range(chunks):
        o32[pl.ds(t, sums, stride=chunks), :] = total[:, t * LANE : (t + 1) * LANE]
    out_ref[:, 0] = o32[...].reshape(devices, o32.shape[0] // devices, LANE).astype(BF16)


def project(core, gathered, w_own, w_peer, tiles):
    devices, per, _ = gathered.shape
    held, width = w_own.shape
    each = 2 * held // LANE
    rows = per // each
    tile = width // 2 // tiles
    chunks = tile // LANE
    w_spec = pl.BlockSpec((held, tile), lambda i, core: (0, core[0] * tiles + i))
    return pl.pallas_call(
        project_kernel,
        grid_spec=pltpu.PrefetchScalarGridSpec(
            num_scalar_prefetch=1,
            grid=(tiles,),
            in_specs=[
                pl.BlockSpec((devices, per, LANE), lambda i, core: (0, 0, 0)),
                w_spec,
                w_spec,
            ],
            out_specs=pl.BlockSpec(
                (devices, 1, rows * chunks, LANE), lambda i, core: (0, i, 0, 0)
            ),
            scratch_shapes=[
                pltpu.VMEM((devices * per, LANE), F32),
                pltpu.VMEM((devices * rows * chunks, LANE), F32),
            ],
        ),
        out_shape=jax.ShapeDtypeStruct((devices, tiles, rows * chunks, LANE), BF16),
        compiler_params=pltpu.CompilerParams(vmem_limit_bytes=14 << 20),
    )(core, gathered, w_own, w_peer)


def norm_kernel(
    cap, slot_ref, sums_ref, hidden_ref, gain_ref, attn_ref, mixed_ref, out_ref, a32, h32, normed
):
    devices, tiles, per, _ = sums_ref.shape
    rows, width = hidden_ref.shape
    chunks = per // rows
    total = width // LANE
    half = total // 2
    for c in range(2):
        for i in range(tiles):
            acc = sums_ref[c, i].astype(F32)
            for k in range(1, devices // 2):
                acc = acc + sums_ref[2 * k + c, i].astype(F32)
            for r in range(rows):
                first = r * total + c * half + i * chunks
                a32[first : first + chunks, :] = acc[r * chunks : (r + 1) * chunks]
    for t in range(total):
        cols = slice(t * LANE, (t + 1) * LANE)
        h32[pl.ds(t, rows, stride=total), :] = hidden_ref[:, cols].astype(F32)
        attn_ref[:, cols] = a32[pl.ds(t, rows, stride=total), :].astype(BF16)
    for r in range(rows):
        span = slice(r * total, (r + 1) * total)
        mixed = h32[span, :] + a32[span, :].astype(BF16).astype(F32)
        mixed_ref[span, :] = mixed
        square = jnp.sum(jnp.sum(mixed * mixed, axis=0, keepdims=True), axis=1, keepdims=True)
        scaled = mixed * lax.rsqrt(square / width + 1e-06) * gain_ref[...]
        normed[2 * r] = scaled[:half].astype(BF16)
        normed[2 * r + 1] = scaled[half:].astype(BF16)
    for e in range(devices // 2):
        for s in range(cap):
            row = slot_ref[e * cap + s]
            for c in range(2):
                out_ref[2 * e + c, s * half : (s + 1) * half, :] = normed[2 * row + c]


def norm_dispatch(slot_rows, sums, hidden_in, mlp_gain, cap):
    devices = sums.shape[0]
    rows, width = hidden_in.shape
    total = width // LANE
    return pl.pallas_call(
        functools.partial(norm_kernel, cap),
        in_specs=[smem_spec(), vmem_spec(), vmem_spec(), vmem_spec()],
        out_specs=[vmem_spec(), vmem_spec(), vmem_spec()],
        out_shape=[
            jax.ShapeDtypeStruct((rows, width), BF16),
            jax.ShapeDtypeStruct((rows * total, LANE), F32),
            jax.ShapeDtypeStruct((devices, cap * total // 2, LANE), BF16),
        ],
        scratch_shapes=[
            pltpu.VMEM((rows * total, LANE), F32),
            pltpu.VMEM((rows * total, LANE), F32),
            pltpu.VMEM((2 * rows, total // 2, LANE), BF16),
        ],
        compiler_params=pltpu.CompilerParams(vmem_limit_bytes=6 << 20),
    )(slot_rows, sums, hidden_in, mlp_gain.reshape(total, LANE))


def expert_kernel(
    core_ref, own_ref, peer_ref, gate_ref, up_ref, down_ref, keep_ref, send_ref, x32, x16
):
    devices, per, _ = own_ref.shape
    core = core_ref[0]
    arrived = x16.shape[1]
    half = x16.shape[2] // LANE
    for index, ref in enumerate((own_ref, peer_ref)):
        x32[...] = ref[...].reshape(devices * per, LANE).astype(F32)
        for t in range(half):
            x16[index, :, t * LANE : (t + 1) * LANE] = x32[
                pl.ds(t, arrived, stride=half), :
            ].astype(BF16)
    depth = half * LANE
    mine = pl.ds(pl.multiple_of(core * depth, depth), depth)
    other = pl.ds(pl.multiple_of((1 - core) * depth, depth), depth)

    def both(w_ref):
        return jnp.dot(x16[0], w_ref[0, mine, :], preferred_element_type=F32) + jnp.dot(
            x16[1], w_ref[0, other, :], preferred_element_type=F32
        )

    gate = both(gate_ref)
    up = both(up_ref)
    act = (gate / (1.0 + jnp.exp(-gate)) * up).astype(BF16)
    for cols, ref in ((other, send_ref), (mine, keep_ref)):
        result = jnp.dot(act, down_ref[0, :, cols], preferred_element_type=F32)
        for t in range(half):
            x32[pl.ds(t, arrived, stride=half), :] = result[:, t * LANE : (t + 1) * LANE]
        ref[...] = x32[...].reshape(devices, per, LANE).astype(BF16)


def experts(core, own, peer, w_gate, w_up, w_down, cap):
    devices, per, _ = own.shape
    half = per // cap
    shape = jax.ShapeDtypeStruct(own.shape, BF16)
    return pl.pallas_call(
        expert_kernel,
        in_specs=[smem_spec()] + [vmem_spec()] * 5,
        out_specs=[vmem_spec()] * 2,
        out_shape=[shape, shape],
        scratch_shapes=[
            pltpu.VMEM((devices * per, LANE), F32),
            pltpu.VMEM((2, devices * cap, half * LANE), BF16),
        ],
        compiler_params=pltpu.CompilerParams(vmem_limit_bytes=24 << 20),
    )(core, own, peer, w_gate, w_up, w_down)


def combine_kernel(cap, place_ref, weight_ref, back_ref, mixed_ref, out_ref, total32):
    rows, width = out_ref.shape
    total = width // LANE
    half = total // 2
    for r in range(rows):
        for c in range(2):
            first = r * total + c * half
            acc = None
            for k in range(place_ref.shape[1]):
                place = place_ref[r, k]
                expert = place // cap
                slot = place - expert * cap
                term = weight_ref[r, k] * back_ref[(2 * expert + c) * cap + slot].astype(F32)
                acc = term if acc is None else acc + term
            total32[first : first + half, :] = mixed_ref[first : first + half, :] + acc
    for t in range(total):
        out_ref[:, t * LANE : (t + 1) * LANE] = total32[pl.ds(t, rows, stride=total), :].astype(
            BF16
        )


def combine(places, route_weight, back, mixed, rows, width, cap):
    return pl.pallas_call(
        functools.partial(combine_kernel, cap),
        in_specs=[smem_spec(), smem_spec(), vmem_spec(), vmem_spec()],
        out_specs=vmem_spec(),
        out_shape=jax.ShapeDtypeStruct((rows, width), BF16),
        scratch_shapes=[pltpu.VMEM(mixed.shape, F32)],
        compiler_params=pltpu.CompilerParams(vmem_limit_bytes=6 << 20),
    )(places, route_weight, back, mixed)


def body(
    hidden_in,
    queries,
    new_kv,
    kv_cache,
    lengths,
    w_out,
    w_gate,
    w_up,
    w_down,
    mlp_gain,
    expert_ids,
    route_weight,
):
    devices = lax.axis_size("node")
    rows, width = hidden_in.shape
    expert_count = devices // 2
    cap = max(2, -(-rows * expert_ids.shape[1] // expert_count))
    core = (lax.axis_index("node") % 2).astype(jnp.int32).reshape(1)
    pairs = [(i, i ^ 1) for i in range(devices)]

    def swap(array):
        return lax.ppermute(array, "node", pairs)

    def exchange(array):
        return lax.all_to_all(array, "node", split_axis=0, concat_axis=0, tiled=True)

    w_peer = swap(w_out)
    context, slot_rows, places = attention(
        queries, new_kv, kv_cache, lengths, expert_ids, devices, cap
    )
    gathered = exchange(context)
    sums = exchange(project(core, gathered, w_out, w_peer, 2))
    attn_out, mixed, outgoing = norm_dispatch(slot_rows, sums, hidden_in, mlp_gain, cap)
    arrived = exchange(outgoing)
    keep, send = experts(core, arrived, swap(arrived), w_gate, w_up, w_down, cap)
    paired = (keep.astype(F32) + swap(send).astype(F32)).astype(BF16)
    back = exchange(paired)
    back = back.reshape(devices * cap, width // 2 // LANE, LANE)
    layer_out = combine(places, route_weight, back, mixed, rows, width, cap)
    return (attn_out, layer_out)


def solution(mesh):
    rows = P(("groups", "node"), None)
    return jax.shard_map(
        body,
        mesh=mesh,
        in_specs=(
            rows,
            rows,
            P(("groups", "node"), None, None),
            P(("groups", "node"), None, None, None),
            P(("groups", "node")),
            P("node", None),
            P("node", None, None),
            P("node", None, None),
            P("node", None, None),
            P(),
            rows,
            rows,
        ),
        out_specs=(rows, rows),
        check_vma=False,
    )
```

```python
import functools
import math

import jax
import jax.numpy as jnp
from jax import lax
from jax.experimental import pallas as pl
from jax.experimental.pallas import tpu as pltpu
from jax.sharding import PartitionSpec as P

HEAD = 128
LANE = 128
F32 = jnp.float32
BF16 = jnp.bfloat16


def vmem_spec():
    return pl.BlockSpec(memory_space=pltpu.VMEM)


def smem_spec():
    return pl.BlockSpec(memory_space=pltpu.SMEM)


def attention_kernel(
    cap,
    core_ref,
    q_hbm,
    new_hbm,
    kv_hbm,
    len_hbm,
    ids_hbm,
    hidden_hbm,
    gain_hbm,
    w_hbm,
    out_ref,
    slot_ref,
    place_ref,
    h32_ref,
    gain_ref,
    keep_ref,
    send_ref,
    qv,
    nv,
    kv,
    hv,
    lens,
    ids,
    q32,
    ctx,
    count,
    sems,
):
    rows, heads, _ = ctx.shape
    experts = slot_ref.shape[0] // cap
    cache_len = kv.shape[2]
    kv_heads = kv.shape[3] // HEAD
    group = heads // kv_heads
    core = core_ref[0]
    half = w_hbm.shape[1] // 2
    mine = pl.ds(pl.multiple_of(core * half, half), half)
    other = pl.ds(pl.multiple_of((1 - core) * half, half), half)
    pairs = [(ids_hbm, ids), (len_hbm, lens), (q_hbm, qv), (new_hbm, nv)]
    pairs += [(kv_hbm.at[r], kv.at[r]) for r in range(rows)]
    pairs += [(hidden_hbm, hv), (gain_hbm, gain_ref)]
    pairs += [(w_hbm.at[:, other], send_ref), (w_hbm.at[:, mine], keep_ref)]
    copies = [
        pltpu.make_async_copy(source, target, sems.at[i])
        for i, (source, target) in enumerate(pairs)
    ]
    for copy in copies:
        copy.start()
    copies[2].wait()
    for h in range(heads):
        q32[pl.ds(h, rows, stride=heads), :] = qv[:, h * HEAD : (h + 1) * HEAD].astype(F32)
    copies[0].wait()
    for e in range(experts):
        count[e] = 0
    for e in range(experts * cap):
        slot_ref[e] = 0
    for row in range(rows):
        for k in range(ids.shape[1]):
            expert = ids[row, k]
            used = count[expert]
            count[expert] = used + 1
            slot_ref[expert * cap + used] = row
            place_ref[row, k] = expert * cap + used
    copies[1].wait()
    copies[3].wait()

    scale = 1.0 / math.sqrt(HEAD)
    spot = lax.broadcasted_iota(jnp.int32, (heads, cache_len), 1)
    batch = 2 if rows % 2 == 0 else 1
    for start in range(0, rows, batch):
        chosen = range(start, start + batch)
        for r in chosen:
            copies[4 + r].wait()
        old, new, value, fresh = [], [], [], []
        for r in chosen:
            query = q32[r * heads : (r + 1) * heads, :]
            parts, fresh_key, fresh_value = [], [], []
            for g in range(kv_heads):
                cols = slice(g * HEAD, (g + 1) * HEAD)
                parts.append(
                    lax.dot_general(
                        query[g * group : (g + 1) * group].astype(BF16),
                        kv[r, 0, :, cols],
                        (((1,), (1,)), ((), ())),
                        preferred_element_type=F32,
                    )
                )
                fresh_key.append(jnp.broadcast_to(nv[r, 0:1, cols].astype(F32), (group, HEAD)))
                fresh_value.append(jnp.broadcast_to(nv[r, 1:2, cols].astype(F32), (group, HEAD)))
            scores = jnp.concatenate(parts, axis=0) * scale
            old.append(jnp.where(spot < lens[r], scores, -jnp.inf))
            new.append(
                jnp.sum(query * jnp.concatenate(fresh_key, axis=0), axis=1, keepdims=True) * scale
            )
            fresh.append(jnp.concatenate(fresh_value, axis=0))
        old = jnp.concatenate(old, axis=0)
        new = jnp.concatenate(new, axis=0)
        top = jnp.maximum(jnp.max(old, axis=1, keepdims=True), new)
        old = jnp.exp(old - top)
        new = jnp.exp(new - top)
        denom = jnp.sum(old, axis=1, keepdims=True) + new
        probs = (old / denom).astype(BF16)
        new = (new / denom).astype(BF16).astype(F32)
        for i, r in enumerate(chosen):
            for g in range(kv_heads):
                first = i * heads + g * group
                value.append(
                    jnp.dot(
                        probs[first : first + group],
                        kv[r, 1, :, g * HEAD : (g + 1) * HEAD],
                        preferred_element_type=F32,
                    )
                )
        result = jnp.concatenate(value, axis=0) + new * jnp.concatenate(fresh, axis=0)
        for i, r in enumerate(chosen):
            ctx[r] = result[i * heads : (i + 1) * heads]

    chips = out_ref.shape[0] // 2
    each = heads // chips
    for i in range(chips):
        block = jnp.concatenate(
            [ctx[r, i * each : (i + 1) * each, :] for r in range(rows)], axis=0
        ).astype(BF16)
        out_ref[2 * i] = block
        out_ref[2 * i + 1] = block
    copies[4 + rows].wait()
    total = h32_ref.shape[0] // rows
    for t in range(total):
        cols = slice(t * LANE, (t + 1) * LANE)
        h32_ref[pl.ds(t, rows, stride=total), :] = hv[:, cols].astype(F32)
    for copy in copies[5 + rows :]:
        copy.wait()


def attention(
    core, queries, new_kv, kv_cache, lengths, expert_ids, hidden_in, gain, w_out, devices, cap
):
    rows, width = hidden_in.shape
    heads = queries.shape[1] // HEAD
    each = heads // (devices // 2)
    experts = devices // 2
    half = jax.ShapeDtypeStruct((w_out.shape[0], width // 2), BF16)
    return pl.pallas_call(
        functools.partial(attention_kernel, cap),
        in_specs=[smem_spec()] + [pl.BlockSpec(memory_space=pltpu.HBM)] * 8,
        out_specs=[vmem_spec(), smem_spec(), smem_spec()] + [vmem_spec()] * 4,
        out_shape=[
            jax.ShapeDtypeStruct((devices, rows * each, LANE), BF16),
            jax.ShapeDtypeStruct((experts * cap,), jnp.int32),
            jax.ShapeDtypeStruct(expert_ids.shape, jnp.int32),
            jax.ShapeDtypeStruct((rows * width // LANE, LANE), F32),
            jax.ShapeDtypeStruct(gain.shape, F32),
            half,
            half,
        ],
        scratch_shapes=[
            pltpu.VMEM(queries.shape, BF16),
            pltpu.VMEM(new_kv.shape, BF16),
            pltpu.VMEM(kv_cache.shape, BF16),
            pltpu.VMEM(hidden_in.shape, BF16),
            pltpu.SMEM(lengths.shape, jnp.int32),
            pltpu.SMEM(expert_ids.shape, jnp.int32),
            pltpu.VMEM((rows * heads, LANE), F32),
            pltpu.VMEM((rows, heads, LANE), F32),
            pltpu.SMEM((experts,), jnp.int32),
            pltpu.SemaphoreType.DMA((8 + rows,)),
        ],
        compiler_params=pltpu.CompilerParams(vmem_limit_bytes=12 << 20),
    )(
        core,
        *(
            pltpu.with_memory_space_constraint(array, pltpu.HBM)
            for array in (
                queries,
                new_kv,
                kv_cache,
                lengths,
                expert_ids,
                hidden_in,
                gain,
                w_out,
            )
        ),
    )


def project_kernel(core_ref, ctx_ref, own_ref, peer_ref, out_ref, x32, o32):
    devices, per, _ = ctx_ref.shape
    x32[...] = ctx_ref[...].reshape(devices * per, LANE).astype(F32)
    core = core_ref[0]
    held, width = own_ref.shape
    each = 2 * held // LANE
    chunks = width // LANE
    sums = o32.shape[0] // chunks

    def left(first):
        return jnp.concatenate(
            [
                x32[pl.ds(first + j, sums, stride=each), :].astype(BF16)
                for j in range(held // LANE)
            ],
            axis=1,
        )

    own_left = left(core * (held // LANE))
    peer_left = left((1 - core) * (held // LANE))
    step = 512
    for first in range(0, width, step):
        cols = slice(first, first + step)
        total = jnp.dot(own_left, own_ref[:, cols], preferred_element_type=F32) + jnp.dot(
            peer_left, peer_ref[:, cols], preferred_element_type=F32
        )
        for t in range(step // LANE):
            o32[pl.ds(first // LANE + t, sums, stride=chunks), :] = total[
                :, t * LANE : (t + 1) * LANE
            ]
    out_ref[:, 0] = o32[...].reshape(devices, o32.shape[0] // devices, LANE).astype(BF16)


def project(core, gathered, w_own, w_peer):
    devices, per, _ = gathered.shape
    held, width = w_own.shape
    rows = per // (2 * held // LANE)
    chunks = width // LANE
    return pl.pallas_call(
        project_kernel,
        in_specs=[smem_spec()] + [vmem_spec()] * 3,
        out_specs=vmem_spec(),
        out_shape=jax.ShapeDtypeStruct((devices, 1, rows * chunks, LANE), BF16),
        scratch_shapes=[
            pltpu.VMEM((devices * per, LANE), F32),
            pltpu.VMEM((devices * rows * chunks, LANE), F32),
        ],
        compiler_params=pltpu.CompilerParams(vmem_limit_bytes=12 << 20),
    )(core, gathered, w_own, w_peer)


def norm_kernel(
    cap, slot_ref, sums_ref, h32_ref, gain_ref, attn_ref, mixed_ref, out_ref, a32, normed
):
    devices, tiles, per, _ = sums_ref.shape
    rows, width = attn_ref.shape
    chunks = per // rows
    total = width // LANE
    half = total // 2
    for c in range(2):
        for i in range(tiles):
            acc = sums_ref[c, i].astype(F32)
            for k in range(1, devices // 2):
                acc = acc + sums_ref[2 * k + c, i].astype(F32)
            for r in range(rows):
                first = r * total + c * half + i * chunks
                a32[first : first + chunks, :] = acc[r * chunks : (r + 1) * chunks]
    for t in range(total):
        cols = slice(t * LANE, (t + 1) * LANE)
        attn_ref[:, cols] = a32[pl.ds(t, rows, stride=total), :].astype(BF16)
    for r in range(rows):
        span = slice(r * total, (r + 1) * total)
        mixed = h32_ref[span, :] + a32[span, :].astype(BF16).astype(F32)
        mixed_ref[span, :] = mixed
        square = jnp.sum(jnp.sum(mixed * mixed, axis=0, keepdims=True), axis=1, keepdims=True)
        scaled = mixed * lax.rsqrt(square / width + 1e-06) * gain_ref[...]
        normed[2 * r] = scaled[:half].astype(BF16)
        normed[2 * r + 1] = scaled[half:].astype(BF16)
    for e in range(devices // 2):
        for s in range(cap):
            row = slot_ref[e * cap + s]
            for c in range(2):
                out_ref[2 * e + c, s * half : (s + 1) * half, :] = normed[2 * row + c]


def norm_dispatch(slot_rows, sums, h32, gain, rows, cap):
    devices = sums.shape[0]
    total = gain.shape[0]
    return pl.pallas_call(
        functools.partial(norm_kernel, cap),
        in_specs=[smem_spec(), vmem_spec(), vmem_spec(), vmem_spec()],
        out_specs=[vmem_spec(), vmem_spec(), vmem_spec()],
        out_shape=[
            jax.ShapeDtypeStruct((rows, total * LANE), BF16),
            jax.ShapeDtypeStruct((rows * total, LANE), F32),
            jax.ShapeDtypeStruct((devices, cap * total // 2, LANE), BF16),
        ],
        scratch_shapes=[
            pltpu.VMEM((rows * total, LANE), F32),
            pltpu.VMEM((2 * rows, total // 2, LANE), BF16),
        ],
        compiler_params=pltpu.CompilerParams(vmem_limit_bytes=6 << 20),
    )(slot_rows, sums, h32, gain)


def expert_kernel(
    core_ref, own_ref, peer_ref, gate_ref, up_ref, down_ref, keep_ref, send_ref, x32, x16
):
    devices, per, _ = own_ref.shape
    core = core_ref[0]
    arrived = x16.shape[1]
    half = x16.shape[2] // LANE
    for index, ref in enumerate((own_ref, peer_ref)):
        x32[...] = ref[...].reshape(devices * per, LANE).astype(F32)
        for t in range(half):
            x16[index, :, t * LANE : (t + 1) * LANE] = x32[
                pl.ds(t, arrived, stride=half), :
            ].astype(BF16)
    depth = half * LANE
    mine = pl.ds(pl.multiple_of(core * depth, depth), depth)
    other = pl.ds(pl.multiple_of((1 - core) * depth, depth), depth)

    def both(w_ref):
        return jnp.dot(x16[0], w_ref[0, mine, :], preferred_element_type=F32) + jnp.dot(
            x16[1], w_ref[0, other, :], preferred_element_type=F32
        )

    gate = both(gate_ref)
    up = both(up_ref)
    act = (gate / (1.0 + jnp.exp(-gate)) * up).astype(BF16)
    for cols, ref in ((other, send_ref), (mine, keep_ref)):
        result = jnp.dot(act, down_ref[0, :, cols], preferred_element_type=F32)
        for t in range(half):
            x32[pl.ds(t, arrived, stride=half), :] = result[:, t * LANE : (t + 1) * LANE]
        ref[...] = x32[...].reshape(devices, per, LANE).astype(BF16)


def experts(core, own, peer, w_gate, w_up, w_down, cap):
    devices, per, _ = own.shape
    half = per // cap
    shape = jax.ShapeDtypeStruct(own.shape, BF16)
    return pl.pallas_call(
        expert_kernel,
        in_specs=[smem_spec()] + [vmem_spec()] * 5,
        out_specs=[vmem_spec()] * 2,
        out_shape=[shape, shape],
        scratch_shapes=[
            pltpu.VMEM((devices * per, LANE), F32),
            pltpu.VMEM((2, devices * cap, half * LANE), BF16),
        ],
        compiler_params=pltpu.CompilerParams(vmem_limit_bytes=24 << 20),
    )(core, own, peer, w_gate, w_up, w_down)


def combine_kernel(cap, place_ref, weight_ref, back_ref, mixed_ref, out_ref, total32):
    rows, width = out_ref.shape
    total = width // LANE
    half = total // 2
    for r in range(rows):
        for c in range(2):
            first = r * total + c * half
            acc = None
            for k in range(place_ref.shape[1]):
                place = place_ref[r, k]
                expert = place // cap
                slot = place - expert * cap
                term = weight_ref[r, k] * back_ref[(2 * expert + c) * cap + slot].astype(F32)
                acc = term if acc is None else acc + term
            total32[first : first + half, :] = mixed_ref[first : first + half, :] + acc
    for t in range(total):
        out_ref[:, t * LANE : (t + 1) * LANE] = total32[pl.ds(t, rows, stride=total), :].astype(
            BF16
        )


def combine(places, route_weight, back, mixed, rows, width, cap):
    return pl.pallas_call(
        functools.partial(combine_kernel, cap),
        in_specs=[smem_spec(), smem_spec(), vmem_spec(), vmem_spec()],
        out_specs=vmem_spec(),
        out_shape=jax.ShapeDtypeStruct((rows, width), BF16),
        scratch_shapes=[pltpu.VMEM(mixed.shape, F32)],
        compiler_params=pltpu.CompilerParams(vmem_limit_bytes=6 << 20),
    )(places, route_weight, back, mixed)


def body(
    hidden_in,
    queries,
    new_kv,
    kv_cache,
    lengths,
    w_out,
    w_gate,
    w_up,
    w_down,
    mlp_gain,
    expert_ids,
    route_weight,
):
    devices = lax.axis_size("node")
    rows, width = hidden_in.shape
    expert_count = devices // 2
    cap = max(2, -(-rows * expert_ids.shape[1] // expert_count))
    core = (lax.axis_index("node") % 2).astype(jnp.int32).reshape(1)
    pairs = [(i, i ^ 1) for i in range(devices)]

    def swap(array):
        return lax.ppermute(array, "node", pairs)

    def exchange(array):
        return lax.all_to_all(array, "node", split_axis=0, concat_axis=0, tiled=True)

    gain = mlp_gain.reshape(width // LANE, LANE)
    context, slot_rows, places, h32, gain, w_keep, w_send = attention(
        core,
        queries,
        new_kv,
        kv_cache,
        lengths,
        expert_ids,
        hidden_in,
        gain,
        w_out,
        devices,
        cap,
    )
    w_peer = swap(w_send)
    gathered = exchange(context)
    sums = exchange(project(core, gathered, w_keep, w_peer))
    attn_out, mixed, outgoing = norm_dispatch(slot_rows, sums, h32, gain, rows, cap)
    arrived = exchange(outgoing)
    keep, send = experts(core, arrived, swap(arrived), w_gate, w_up, w_down, cap)
    paired = (keep.astype(F32) + swap(send).astype(F32)).astype(BF16)
    back = exchange(paired)
    back = back.reshape(devices * cap, width // 2 // LANE, LANE)
    layer_out = combine(places, route_weight, back, mixed, rows, width, cap)
    return (attn_out, layer_out)


def solution(mesh):
    rows = P(("groups", "node"), None)
    return jax.shard_map(
        body,
        mesh=mesh,
        in_specs=(
            rows,
            rows,
            P(("groups", "node"), None, None),
            P(("groups", "node"), None, None, None),
            P(("groups", "node")),
            P("node", None),
            P("node", None, None),
            P("node", None, None),
            P("node", None, None),
            P(),
            rows,
            rows,
        ),
        out_specs=(rows, rows),
        check_vma=False,
    )
```

```python
import functools
import math

import jax
import jax.numpy as jnp
from jax import lax
from jax.experimental import pallas as pl
from jax.experimental.pallas import tpu as pltpu
from jax.sharding import PartitionSpec as P

HEAD = 128
LANE = 128
F32 = jnp.float32
BF16 = jnp.bfloat16


def vmem_spec():
    return pl.BlockSpec(memory_space=pltpu.VMEM)


def attention_kernel(
    cap,
    q_hbm,
    new_hbm,
    kv_hbm,
    len_hbm,
    ids_hbm,
    route_hbm,
    hidden_hbm,
    gain_hbm,
    w_hbm,
    out_ref,
    weight_ref,
    pick_ref,
    h32_ref,
    gain_ref,
    keep_ref,
    send_ref,
    qv,
    nv,
    kv,
    hv,
    lens,
    ids,
    route,
    q32,
    ctx,
    count,
    sems,
):
    rows, heads, _ = ctx.shape
    slots = weight_ref.shape[0] // rows
    cache_len = kv.shape[2]
    kv_heads = kv.shape[3] // HEAD
    group = heads // kv_heads
    core = lax.axis_index("node") % 2
    half = w_hbm.shape[1] // 2
    mine = pl.ds(pl.multiple_of(core * half, half), half)
    other = pl.ds(pl.multiple_of((1 - core) * half, half), half)
    pairs = [(ids_hbm, ids), (len_hbm, lens), (q_hbm, qv), (new_hbm, nv)]
    pairs += [(kv_hbm.at[r], kv.at[r]) for r in range(rows)]
    pairs += [(hidden_hbm, hv), (gain_hbm, gain_ref), (route_hbm, route)]
    pairs += [(w_hbm.at[:, other], send_ref), (w_hbm.at[:, mine], keep_ref)]
    copies = [
        pltpu.make_async_copy(source, target, sems.at[i])
        for i, (source, target) in enumerate(pairs)
    ]
    for copy in copies:
        copy.start()
    copies[2].wait()
    for h in range(heads):
        q32[pl.ds(h, rows, stride=heads), :] = qv[:, h * HEAD : (h + 1) * HEAD].astype(F32)
    weight_ref[...] = jnp.zeros(weight_ref.shape, F32)
    pick_ref[...] = jnp.zeros(pick_ref.shape, F32)
    for e in range(slots // cap):
        count[e] = 0
    copies[0].wait()
    copies[6 + rows].wait()
    for row in range(rows):
        for k in range(ids.shape[1]):
            expert = ids[row, k]
            used = count[expert]
            count[expert] = used + 1
            slot = expert * cap + used
            weight_ref[pl.ds(row * slots + slot, 1), :] = jnp.full((1, LANE), route[row, k], F32)
            pick_ref[pl.ds(slot * rows + row, 1), :] = jnp.ones((1, LANE), F32)
    copies[1].wait()
    copies[3].wait()

    scale = 1.0 / math.sqrt(HEAD)
    spot = lax.broadcasted_iota(jnp.int32, (heads, cache_len), 1)
    batch = 2 if rows % 2 == 0 else 1
    for start in range(0, rows, batch):
        chosen = range(start, start + batch)
        for r in chosen:
            copies[4 + r].wait()
        old, new, value, fresh = [], [], [], []
        for r in chosen:
            query = q32[r * heads : (r + 1) * heads, :]
            parts, fresh_key, fresh_value = [], [], []
            for g in range(kv_heads):
                cols = slice(g * HEAD, (g + 1) * HEAD)
                parts.append(
                    lax.dot_general(
                        query[g * group : (g + 1) * group].astype(BF16),
                        kv[r, 0, :, cols],
                        (((1,), (1,)), ((), ())),
                        preferred_element_type=F32,
                    )
                )
                fresh_key.append(jnp.broadcast_to(nv[r, 0:1, cols].astype(F32), (group, HEAD)))
                fresh_value.append(jnp.broadcast_to(nv[r, 1:2, cols].astype(F32), (group, HEAD)))
            scores = jnp.concatenate(parts, axis=0) * scale
            old.append(jnp.where(spot < lens[r], scores, -jnp.inf))
            new.append(
                jnp.sum(query * jnp.concatenate(fresh_key, axis=0), axis=1, keepdims=True) * scale
            )
            fresh.append(jnp.concatenate(fresh_value, axis=0))
        old = jnp.concatenate(old, axis=0)
        new = jnp.concatenate(new, axis=0)
        top = jnp.maximum(jnp.max(old, axis=1, keepdims=True), new)
        old = jnp.exp(old - top)
        new = jnp.exp(new - top)
        denom = jnp.sum(old, axis=1, keepdims=True) + new
        probs = (old / denom).astype(BF16)
        new = (new / denom).astype(BF16).astype(F32)
        for i, r in enumerate(chosen):
            for g in range(kv_heads):
                first = i * heads + g * group
                value.append(
                    jnp.dot(
                        probs[first : first + group],
                        kv[r, 1, :, g * HEAD : (g + 1) * HEAD],
                        preferred_element_type=F32,
                    )
                )
        result = jnp.concatenate(value, axis=0) + new * jnp.concatenate(fresh, axis=0)
        for i, r in enumerate(chosen):
            ctx[r] = result[i * heads : (i + 1) * heads]

    chips = out_ref.shape[0] // 2
    each = heads // chips
    for i in range(chips):
        block = jnp.concatenate(
            [ctx[r, i * each : (i + 1) * each, :] for r in range(rows)], axis=0
        ).astype(BF16)
        out_ref[2 * i] = block
        out_ref[2 * i + 1] = block
    copies[4 + rows].wait()
    total = h32_ref.shape[0] // rows
    for t in range(total):
        cols = slice(t * LANE, (t + 1) * LANE)
        h32_ref[pl.ds(t, rows, stride=total), :] = hv[:, cols].astype(F32)
    copies[5 + rows].wait()
    for copy in copies[7 + rows :]:
        copy.wait()


def attention(
    queries, new_kv, kv_cache, lengths, expert_ids, route_weight, hidden_in, gain, w_out, devices, cap
):
    rows, width = hidden_in.shape
    heads = queries.shape[1] // HEAD
    each = heads // (devices // 2)
    experts = devices // 2
    half = jax.ShapeDtypeStruct((w_out.shape[0], width // 2), BF16)
    table = jax.ShapeDtypeStruct((rows * experts * cap, LANE), F32)
    arrays = (
        queries,
        new_kv,
        kv_cache,
        lengths,
        expert_ids,
        route_weight,
        hidden_in,
        gain,
        w_out,
    )
    return pl.pallas_call(
        functools.partial(attention_kernel, cap),
        in_specs=[pl.BlockSpec(memory_space=pltpu.HBM)] * len(arrays),
        out_specs=[vmem_spec()] * 7,
        out_shape=[
            jax.ShapeDtypeStruct((devices, rows * each, LANE), BF16),
            table,
            table,
            jax.ShapeDtypeStruct((rows * width // LANE, LANE), F32),
            jax.ShapeDtypeStruct(gain.shape, F32),
            half,
            half,
        ],
        scratch_shapes=[
            pltpu.VMEM(queries.shape, BF16),
            pltpu.VMEM(new_kv.shape, BF16),
            pltpu.VMEM(kv_cache.shape, BF16),
            pltpu.VMEM(hidden_in.shape, BF16),
            pltpu.SMEM(lengths.shape, jnp.int32),
            pltpu.SMEM(expert_ids.shape, jnp.int32),
            pltpu.SMEM(route_weight.shape, F32),
            pltpu.VMEM((rows * heads, LANE), F32),
            pltpu.VMEM((rows, heads, LANE), F32),
            pltpu.SMEM((experts,), jnp.int32),
            pltpu.SemaphoreType.DMA((9 + rows,)),
        ],
        compiler_params=pltpu.CompilerParams(vmem_limit_bytes=12 << 20),
    )(*(pltpu.with_memory_space_constraint(array, pltpu.HBM) for array in arrays))


def project_kernel(ctx_ref, own_ref, peer_ref, out_ref, x32, o32):
    devices, per, _ = ctx_ref.shape
    x32[...] = ctx_ref[...].reshape(devices * per, LANE).astype(F32)
    core = lax.axis_index("node") % 2
    held, width = own_ref.shape
    each = 2 * held // LANE
    chunks = width // LANE
    sums = o32.shape[0] // chunks

    def left(first):
        return jnp.concatenate(
            [
                x32[pl.ds(first + j, sums, stride=each), :].astype(BF16)
                for j in range(held // LANE)
            ],
            axis=1,
        )

    own_left = left(core * (held // LANE))
    peer_left = left((1 - core) * (held // LANE))
    step = 512
    for first in range(0, width, step):
        cols = slice(first, first + step)
        total = jnp.dot(own_left, own_ref[:, cols], preferred_element_type=F32) + jnp.dot(
            peer_left, peer_ref[:, cols], preferred_element_type=F32
        )
        for t in range(step // LANE):
            o32[pl.ds(first // LANE + t, sums, stride=chunks), :] = total[
                :, t * LANE : (t + 1) * LANE
            ]
    out_ref[:, 0] = o32[...].reshape(devices, o32.shape[0] // devices, LANE).astype(BF16)


def project(gathered, w_own, w_peer):
    devices, per, _ = gathered.shape
    held, width = w_own.shape
    rows = per // (2 * held // LANE)
    chunks = width // LANE
    return pl.pallas_call(
        project_kernel,
        in_specs=[vmem_spec()] * 3,
        out_specs=vmem_spec(),
        out_shape=jax.ShapeDtypeStruct((devices, 1, rows * chunks, LANE), BF16),
        scratch_shapes=[
            pltpu.VMEM((devices * per, LANE), F32),
            pltpu.VMEM((devices * rows * chunks, LANE), F32),
        ],
        compiler_params=pltpu.CompilerParams(vmem_limit_bytes=12 << 20),
    )(gathered, w_own, w_peer)


def norm_kernel(cap, sums_ref, h32_ref, gain_ref, pick_ref, attn_ref, mixed_ref, out_ref):
    devices, tiles, per, _ = sums_ref.shape
    total = gain_ref.shape[0]
    rows = h32_ref.shape[0] // total
    half = total // 2
    for c in range(2):
        acc = sums_ref[c, 0].astype(F32)
        for k in range(1, devices // 2):
            acc = acc + sums_ref[2 * k + c, 0].astype(F32)
        for r in range(rows):
            attn_ref[r * total + c * half : r * total + (c + 1) * half, :] = acc[
                r * half : (r + 1) * half
            ]
    normed = []
    for r in range(rows):
        span = slice(r * total, (r + 1) * total)
        mixed = h32_ref[span, :] + attn_ref[span, :].astype(BF16).astype(F32)
        mixed_ref[span, :] = mixed
        square = jnp.sum(jnp.sum(mixed * mixed, axis=0, keepdims=True), axis=1, keepdims=True)
        scaled = mixed * lax.rsqrt(square / width_of(total) + 1e-06) * gain_ref[...]
        normed.append(scaled)
    for slot in range(devices // 2 * cap):
        e, s = divmod(slot, cap)
        chosen = normed[0] * pick_ref[slot * rows : slot * rows + 1, :]
        for r in range(1, rows):
            chosen = chosen + normed[r] * pick_ref[slot * rows + r : slot * rows + r + 1, :]
        chosen = chosen.astype(BF16)
        for c in range(2):
            out_ref[2 * e + c, s * half : (s + 1) * half, :] = chosen[c * half : (c + 1) * half]


def width_of(chunks):
    return chunks * LANE


def norm_dispatch(sums, h32, gain, pick, cap):
    devices = sums.shape[0]
    total = gain.shape[0]
    state = jax.ShapeDtypeStruct(h32.shape, F32)
    return pl.pallas_call(
        functools.partial(norm_kernel, cap),
        in_specs=[vmem_spec()] * 4,
        out_specs=[vmem_spec()] * 3,
        out_shape=[
            state,
            state,
            jax.ShapeDtypeStruct((devices, cap * total // 2, LANE), BF16),
        ],
        compiler_params=pltpu.CompilerParams(vmem_limit_bytes=6 << 20),
    )(sums, h32, gain, pick)


def rows_from_chunks(ref, x32, x16):
    devices, per, _ = ref.shape
    arrived, width = x16.shape
    half = width // LANE
    x32[...] = ref[...].reshape(devices * per, LANE).astype(F32)
    for t in range(half):
        x16[:, t * LANE : (t + 1) * LANE] = x32[pl.ds(t, arrived, stride=half), :].astype(BF16)


def chunks_from_rows(result, x32, ref):
    arrived, width = result.shape
    half = width // LANE
    for t in range(half):
        x32[pl.ds(t, arrived, stride=half), :] = result[:, t * LANE : (t + 1) * LANE]
    ref[...] = x32[...].reshape(ref.shape).astype(BF16)


def half_of(which, size):
    return pl.ds(pl.multiple_of(which * size, size), size)


def own_kernel(own_ref, gate_ref, up_ref, gate_out, up_out, x32, x16):
    rows_from_chunks(own_ref, x32, x16)
    span = half_of(lax.axis_index("node") % 2, x16.shape[1])
    gate_out[...] = jnp.dot(x16[...], gate_ref[0, span, :], preferred_element_type=F32)
    up_out[...] = jnp.dot(x16[...], up_ref[0, span, :], preferred_element_type=F32)


def peer_kernel(
    peer_ref, gate_in, up_in, gate_ref, up_ref, down_ref, act_ref, send_ref, x32, x16
):
    rows_from_chunks(peer_ref, x32, x16)
    span = half_of(1 - lax.axis_index("node") % 2, x16.shape[1])
    gate = gate_in[...] + jnp.dot(x16[...], gate_ref[0, span, :], preferred_element_type=F32)
    up = up_in[...] + jnp.dot(x16[...], up_ref[0, span, :], preferred_element_type=F32)
    act = (gate / (1.0 + jnp.exp(-gate)) * up).astype(BF16)
    act_ref[...] = act
    result = jnp.dot(act, down_ref[0, :, span], preferred_element_type=F32)
    chunks_from_rows(result, x32, send_ref)


def keep_kernel(act_ref, down_ref, keep_ref, x32):
    size = down_ref.shape[2] // 2
    span = half_of(lax.axis_index("node") % 2, size)
    result = jnp.dot(act_ref[...], down_ref[0, :, span], preferred_element_type=F32)
    chunks_from_rows(result, x32, keep_ref)


def estimate(flops, moved):
    return pl.CostEstimate(flops=flops, bytes_accessed=moved, transcendentals=0)


def experts(own, swap, w_gate, w_up, w_down, cap):
    devices, per, _ = own.shape
    half = per // cap * LANE
    arrived = devices * cap
    hidden = w_gate.shape[2]
    chunked = jax.ShapeDtypeStruct(own.shape, BF16)
    sums = jax.ShapeDtypeStruct((arrived, hidden), F32)
    wide = pltpu.VMEM((devices * per, LANE), F32)
    narrow = pltpu.VMEM((arrived, half), BF16)
    params = pltpu.CompilerParams(vmem_limit_bytes=8 << 20)
    peer = swap(own)
    gate, up = pl.pallas_call(
        own_kernel,
        in_specs=[vmem_spec()] * 3,
        out_specs=[vmem_spec()] * 2,
        out_shape=[sums, sums],
        scratch_shapes=[wide, narrow],
        compiler_params=params,
        cost_estimate=estimate(4 * arrived * half * hidden, 4 * half * hidden),
    )(own, w_gate, w_up)
    act, send = pl.pallas_call(
        peer_kernel,
        in_specs=[vmem_spec()] * 6,
        out_specs=[vmem_spec()] * 2,
        out_shape=[jax.ShapeDtypeStruct((arrived, hidden), BF16), chunked],
        scratch_shapes=[wide, narrow],
        compiler_params=params,
        cost_estimate=estimate(6 * arrived * half * hidden, 6 * half * hidden),
    )(peer, gate, up, w_gate, w_up, w_down)
    received = swap(send)
    keep = pl.pallas_call(
        keep_kernel,
        in_specs=[vmem_spec()] * 2,
        out_specs=vmem_spec(),
        out_shape=chunked,
        scratch_shapes=[wide],
        compiler_params=params,
        cost_estimate=estimate(2 * arrived * half * hidden, 2 * half * hidden),
    )(act, w_down)
    return (keep.astype(F32) + received.astype(F32)).astype(BF16)


def combine_kernel(cap, weight_ref, back_ref, mixed_ref, a32_ref, attn_ref, out_ref, total32):
    rows, width = out_ref.shape
    total = width // LANE
    half = total // 2
    slots = weight_ref.shape[0] // rows
    for t in range(total):
        cols = slice(t * LANE, (t + 1) * LANE)
        attn_ref[:, cols] = a32_ref[pl.ds(t, rows, stride=total), :].astype(BF16)
    for c in range(2):
        acc = [
            mixed_ref[r * total + c * half : r * total + (c + 1) * half, :] for r in range(rows)
        ]
        for slot in range(slots):
            e, s = divmod(slot, cap)
            block = back_ref[2 * e + c, s * half : (s + 1) * half, :].astype(F32)
            for r in range(rows):
                acc[r] = acc[r] + weight_ref[r * slots + slot : r * slots + slot + 1, :] * block
        for r in range(rows):
            total32[r * total + c * half : r * total + (c + 1) * half, :] = acc[r]
    for t in range(total):
        out_ref[:, t * LANE : (t + 1) * LANE] = total32[pl.ds(t, rows, stride=total), :].astype(
            BF16
        )


def combine(weights, back, mixed, a32, rows, width, cap):
    shape = jax.ShapeDtypeStruct((rows, width), BF16)
    return pl.pallas_call(
        functools.partial(combine_kernel, cap),
        in_specs=[vmem_spec()] * 4,
        out_specs=[vmem_spec()] * 2,
        out_shape=[shape, shape],
        scratch_shapes=[pltpu.VMEM(mixed.shape, F32)],
        compiler_params=pltpu.CompilerParams(vmem_limit_bytes=6 << 20),
    )(weights, back, mixed, a32)


def body(
    hidden_in,
    queries,
    new_kv,
    kv_cache,
    lengths,
    w_out,
    w_gate,
    w_up,
    w_down,
    mlp_gain,
    expert_ids,
    route_weight,
):
    devices = lax.axis_size("node")
    rows, width = hidden_in.shape
    expert_count = devices // 2
    cap = max(2, -(-rows * expert_ids.shape[1] // expert_count))
    pairs = [(i, i ^ 1) for i in range(devices)]

    def swap(array):
        return lax.ppermute(array, "node", pairs)

    def exchange(array):
        return lax.all_to_all(array, "node", split_axis=0, concat_axis=0, tiled=True)

    gain = mlp_gain.reshape(width // LANE, LANE)
    context, weights, pick, h32, gain, w_keep, w_send = attention(
        queries,
        new_kv,
        kv_cache,
        lengths,
        expert_ids,
        route_weight,
        hidden_in,
        gain,
        w_out,
        devices,
        cap,
    )
    w_peer = swap(w_send)
    gathered = exchange(context)
    sums = exchange(project(gathered, w_keep, w_peer))
    a32, mixed, outgoing = norm_dispatch(sums, h32, gain, pick, cap)
    arrived = exchange(outgoing)
    back = exchange(experts(arrived, swap, w_gate, w_up, w_down, cap))
    return combine(weights, back, mixed, a32, rows, width, cap)


def solution(mesh):
    rows = P(("groups", "node"), None)
    return jax.shard_map(
        body,
        mesh=mesh,
        in_specs=(
            rows,
            rows,
            P(("groups", "node"), None, None),
            P(("groups", "node"), None, None, None),
            P(("groups", "node")),
            P("node", None),
            P("node", None, None),
            P("node", None, None),
            P("node", None, None),
            P(),
            rows,
            rows,
        ),
        out_specs=(rows, rows),
        check_vma=False,
    )
```

```python
import functools
import math

import jax
import jax.numpy as jnp
from jax import lax
from jax.experimental import pallas as pl
from jax.experimental.pallas import tpu as pltpu
from jax.sharding import PartitionSpec as P

HEAD = 128
LANE = 128
F32 = jnp.float32
BF16 = jnp.bfloat16


def vmem_spec():
    return pl.BlockSpec(memory_space=pltpu.VMEM)


def attention_kernel(
    cap,
    q_hbm,
    new_hbm,
    kv_hbm,
    len_hbm,
    ids_hbm,
    route_hbm,
    hidden_hbm,
    gain_hbm,
    w_hbm,
    out_ref,
    weight_ref,
    pick_ref,
    h32_ref,
    gain_ref,
    keep_ref,
    qv,
    nv,
    kv,
    hv,
    lens,
    ids,
    route,
    q32,
    ctx,
    count,
    sems,
):
    rows, heads, _ = ctx.shape
    slots = weight_ref.shape[0] // rows
    cache_len = kv.shape[2]
    kv_heads = kv.shape[3] // HEAD
    group = heads // kv_heads
    core = lax.axis_index("node") % 2
    half = w_hbm.shape[1] // 2
    mine = pl.ds(pl.multiple_of(core * half, half), half)
    pairs = [(ids_hbm, ids), (len_hbm, lens), (q_hbm, qv), (new_hbm, nv)]
    pairs += [(kv_hbm.at[r], kv.at[r]) for r in range(rows)]
    pairs += [(hidden_hbm, hv), (gain_hbm, gain_ref), (route_hbm, route)]
    pairs += [(w_hbm.at[:, mine], keep_ref)]
    copies = [
        pltpu.make_async_copy(source, target, sems.at[i])
        for i, (source, target) in enumerate(pairs)
    ]
    for copy in copies[: 7 + rows]:
        copy.start()
    copies[2].wait()
    for copy in copies[7 + rows :]:
        copy.start()
    for h in range(heads):
        q32[pl.ds(h, rows, stride=heads), :] = qv[:, h * HEAD : (h + 1) * HEAD].astype(F32)
    weight_ref[...] = jnp.zeros(weight_ref.shape, F32)
    pick_ref[...] = jnp.zeros(pick_ref.shape, F32)
    for e in range(slots // cap):
        count[e] = 0
    copies[0].wait()
    copies[6 + rows].wait()
    for row in range(rows):
        for k in range(ids.shape[1]):
            expert = ids[row, k]
            used = count[expert]
            count[expert] = used + 1
            slot = expert * cap + used
            weight_ref[pl.ds(row * slots + slot, 1), :] = jnp.full((1, LANE), route[row, k], F32)
            pick_ref[pl.ds(slot * rows + row, 1), :] = jnp.ones((1, LANE), F32)
    copies[1].wait()
    copies[3].wait()

    scale = 1.0 / math.sqrt(HEAD)
    spot = lax.broadcasted_iota(jnp.int32, (heads, cache_len), 1)
    batch = rows
    for start in range(0, rows, batch):
        chosen = range(start, start + batch)
        for r in chosen:
            copies[4 + r].wait()
        old, new, value, fresh = [], [], [], []
        for r in chosen:
            query = q32[r * heads : (r + 1) * heads, :]
            parts, fresh_key, fresh_value = [], [], []
            for g in range(kv_heads):
                cols = slice(g * HEAD, (g + 1) * HEAD)
                parts.append(
                    lax.dot_general(
                        query[g * group : (g + 1) * group].astype(BF16),
                        kv[r, 0, :, cols],
                        (((1,), (1,)), ((), ())),
                        preferred_element_type=F32,
                    )
                )
                fresh_key.append(jnp.broadcast_to(nv[r, 0:1, cols].astype(F32), (group, HEAD)))
                fresh_value.append(jnp.broadcast_to(nv[r, 1:2, cols].astype(F32), (group, HEAD)))
            scores = jnp.concatenate(parts, axis=0) * scale
            old.append(jnp.where(spot < lens[r], scores, -jnp.inf))
            new.append(
                jnp.sum(query * jnp.concatenate(fresh_key, axis=0), axis=1, keepdims=True) * scale
            )
            fresh.append(jnp.concatenate(fresh_value, axis=0))
        old = jnp.concatenate(old, axis=0)
        new = jnp.concatenate(new, axis=0)
        top = jnp.maximum(jnp.max(old, axis=1, keepdims=True), new)
        old = jnp.exp(old - top)
        new = jnp.exp(new - top)
        share = 1.0 / (jnp.sum(old, axis=1, keepdims=True) + new)
        probs = (old * share).astype(BF16)
        new = (new * share).astype(BF16).astype(F32)
        for i, r in enumerate(chosen):
            for g in range(kv_heads):
                first = i * heads + g * group
                value.append(
                    jnp.dot(
                        probs[first : first + group],
                        kv[r, 1, :, g * HEAD : (g + 1) * HEAD],
                        preferred_element_type=F32,
                    )
                )
        result = jnp.concatenate(value, axis=0) + new * jnp.concatenate(fresh, axis=0)
        for i, r in enumerate(chosen):
            ctx[r] = result[i * heads : (i + 1) * heads]

    chips = out_ref.shape[0] // 2
    each = heads // chips
    for i in range(chips):
        block = jnp.concatenate(
            [ctx[r, i * each : (i + 1) * each, :] for r in range(rows)], axis=0
        ).astype(BF16)
        out_ref[2 * i] = block
        out_ref[2 * i + 1] = block
    copies[4 + rows].wait()
    total = h32_ref.shape[0] // rows
    for t in range(total):
        cols = slice(t * LANE, (t + 1) * LANE)
        h32_ref[pl.ds(t, rows, stride=total), :] = hv[:, cols].astype(F32)
    copies[5 + rows].wait()
    for copy in copies[7 + rows :]:
        copy.wait()


def attention(
    queries, new_kv, kv_cache, lengths, expert_ids, route_weight, hidden_in, gain, w_out, devices, cap
):
    rows, width = hidden_in.shape
    heads = queries.shape[1] // HEAD
    each = heads // (devices // 2)
    experts = devices // 2
    half = jax.ShapeDtypeStruct((w_out.shape[0], width // 2), BF16)
    table = jax.ShapeDtypeStruct((rows * experts * cap, LANE), F32)
    arrays = (
        queries,
        new_kv,
        kv_cache,
        lengths,
        expert_ids,
        route_weight,
        hidden_in,
        gain,
        w_out,
    )
    return pl.pallas_call(
        functools.partial(attention_kernel, cap),
        in_specs=[pl.BlockSpec(memory_space=pltpu.HBM)] * len(arrays),
        out_specs=[vmem_spec()] * 6,
        out_shape=[
            jax.ShapeDtypeStruct((devices, rows * each, LANE), BF16),
            table,
            table,
            jax.ShapeDtypeStruct((rows * width // LANE, LANE), F32),
            jax.ShapeDtypeStruct(gain.shape, F32),
            half,
        ],
        scratch_shapes=[
            pltpu.VMEM(queries.shape, BF16),
            pltpu.VMEM(new_kv.shape, BF16),
            pltpu.VMEM(kv_cache.shape, BF16),
            pltpu.VMEM(hidden_in.shape, BF16),
            pltpu.SMEM(lengths.shape, jnp.int32),
            pltpu.SMEM(expert_ids.shape, jnp.int32),
            pltpu.SMEM(route_weight.shape, F32),
            pltpu.VMEM((rows * heads, LANE), F32),
            pltpu.VMEM((rows, heads, LANE), F32),
            pltpu.SMEM((experts,), jnp.int32),
            pltpu.SemaphoreType.DMA((8 + rows,)),
        ],
        compiler_params=pltpu.CompilerParams(vmem_limit_bytes=12 << 20),
    )(*(pltpu.with_memory_space_constraint(array, pltpu.HBM) for array in arrays))


def project_kernel(ctx_ref, own_ref, peer_ref, out_ref, x32, o32):
    devices, per, _ = ctx_ref.shape
    x32[...] = ctx_ref[...].reshape(devices * per, LANE).astype(F32)
    core = lax.axis_index("node") % 2
    held, width = own_ref.shape
    each = 2 * held // LANE
    chunks = width // LANE
    sums = o32.shape[0] // chunks

    def left(first):
        return jnp.concatenate(
            [
                x32[pl.ds(first + j, sums, stride=each), :].astype(BF16)
                for j in range(held // LANE)
            ],
            axis=1,
        )

    def half_cols(first, step):
        return pl.ds(pl.multiple_of(core * width + first, LANE), step)

    own_left = left(core * (held // LANE))
    peer_left = left((1 - core) * (held // LANE))
    step = 512
    for first in range(0, width, step):
        cols = slice(first, first + step)
        total = jnp.dot(own_left, own_ref[:, cols], preferred_element_type=F32) + jnp.dot(
            peer_left, peer_ref[:, half_cols(first, step)], preferred_element_type=F32
        )
        for t in range(step // LANE):
            o32[pl.ds(first // LANE + t, sums, stride=chunks), :] = total[
                :, t * LANE : (t + 1) * LANE
            ]
    out_ref[:, 0] = o32[...].reshape(devices, o32.shape[0] // devices, LANE).astype(BF16)


def project(gathered, w_own, w_peer):
    devices, per, _ = gathered.shape
    held, width = w_own.shape
    rows = per // (2 * held // LANE)
    chunks = width // LANE
    return pl.pallas_call(
        project_kernel,
        in_specs=[vmem_spec()] * 3,
        out_specs=vmem_spec(),
        out_shape=jax.ShapeDtypeStruct((devices, 1, rows * chunks, LANE), BF16),
        scratch_shapes=[
            pltpu.VMEM((devices * per, LANE), F32),
            pltpu.VMEM((devices * rows * chunks, LANE), F32),
        ],
        compiler_params=pltpu.CompilerParams(vmem_limit_bytes=12 << 20),
    )(gathered, w_own, w_peer)


def norm_kernel(cap, sums_ref, h32_ref, gain_ref, pick_ref, attn_ref, mixed_ref, out_ref):
    devices, tiles, per, _ = sums_ref.shape
    total = gain_ref.shape[0]
    rows = h32_ref.shape[0] // total
    half = total // 2
    for c in range(2):
        acc = sums_ref[c, 0].astype(F32)
        for k in range(1, devices // 2):
            acc = acc + sums_ref[2 * k + c, 0].astype(F32)
        for r in range(rows):
            attn_ref[r * total + c * half : r * total + (c + 1) * half, :] = acc[
                r * half : (r + 1) * half
            ]
    normed = []
    for r in range(rows):
        span = slice(r * total, (r + 1) * total)
        mixed = h32_ref[span, :] + attn_ref[span, :].astype(BF16).astype(F32)
        mixed_ref[span, :] = mixed
        square = jnp.sum(jnp.sum(mixed * mixed, axis=0, keepdims=True), axis=1, keepdims=True)
        scaled = mixed * lax.rsqrt(square / width_of(total) + 1e-06) * gain_ref[...]
        normed.append(scaled)
    for slot in range(devices // 2 * cap):
        e, s = divmod(slot, cap)
        chosen = normed[0] * pick_ref[slot * rows : slot * rows + 1, :]
        for r in range(1, rows):
            chosen = chosen + normed[r] * pick_ref[slot * rows + r : slot * rows + r + 1, :]
        chosen = chosen.astype(BF16)
        for c in range(2):
            out_ref[2 * e + c, s * half : (s + 1) * half, :] = chosen[c * half : (c + 1) * half]


def width_of(chunks):
    return chunks * LANE


def norm_dispatch(sums, h32, gain, pick, cap):
    devices = sums.shape[0]
    total = gain.shape[0]
    state = jax.ShapeDtypeStruct(h32.shape, F32)
    return pl.pallas_call(
        functools.partial(norm_kernel, cap),
        in_specs=[vmem_spec()] * 4,
        out_specs=[vmem_spec()] * 3,
        out_shape=[
            state,
            state,
            jax.ShapeDtypeStruct((devices, cap * total // 2, LANE), BF16),
        ],
        compiler_params=pltpu.CompilerParams(vmem_limit_bytes=6 << 20),
    )(sums, h32, gain, pick)


def rows_from_chunks(ref, x32, x16):
    devices, per, _ = ref.shape
    arrived, width = x16.shape
    half = width // LANE
    x32[...] = ref[...].reshape(devices * per, LANE).astype(F32)
    for t in range(half):
        x16[:, t * LANE : (t + 1) * LANE] = x32[pl.ds(t, arrived, stride=half), :].astype(BF16)


def chunks_from_rows(result, x32, ref):
    arrived, width = result.shape
    half = width // LANE
    for t in range(half):
        x32[pl.ds(t, arrived, stride=half), :] = result[:, t * LANE : (t + 1) * LANE]
    ref[...] = x32[...].reshape(ref.shape).astype(BF16)


def half_of(which, size):
    return pl.ds(pl.multiple_of(which * size, size), size)


def own_kernel(own_ref, gate_ref, up_ref, down_ref, gate_out, up_out, x32, x16):
    rows_from_chunks(own_ref, x32, x16)
    span = half_of(lax.axis_index("node") % 2, x16.shape[1])
    gate_out[...] = jnp.dot(x16[...], gate_ref[0, span, :], preferred_element_type=F32)
    up_out[...] = jnp.dot(x16[...], up_ref[0, span, :], preferred_element_type=F32)


def peer_kernel(
    peer_ref, gate_in, up_in, gate_ref, up_ref, down_ref, act_ref, send_ref, x32, x16
):
    rows_from_chunks(peer_ref, x32, x16)
    span = half_of(1 - lax.axis_index("node") % 2, x16.shape[1])
    gate = gate_in[...] + jnp.dot(x16[...], gate_ref[0, span, :], preferred_element_type=F32)
    up = up_in[...] + jnp.dot(x16[...], up_ref[0, span, :], preferred_element_type=F32)
    act = (gate / (1.0 + jnp.exp(-gate)) * up).astype(BF16)
    act_ref[...] = act
    result = jnp.dot(act, down_ref[0, :, span], preferred_element_type=F32)
    chunks_from_rows(result, x32, send_ref)


def keep_kernel(act_ref, down_ref, keep_ref, x32):
    size = down_ref.shape[2] // 2
    span = half_of(lax.axis_index("node") % 2, size)
    result = jnp.dot(act_ref[...], down_ref[0, :, span], preferred_element_type=F32)
    chunks_from_rows(result, x32, keep_ref)


def estimate(flops, moved):
    return pl.CostEstimate(flops=flops, bytes_accessed=moved, transcendentals=0)


def experts(own, swap, w_gate, w_up, w_down, cap):
    devices, per, _ = own.shape
    half = per // cap * LANE
    arrived = devices * cap
    hidden = w_gate.shape[2]
    chunked = jax.ShapeDtypeStruct(own.shape, BF16)
    sums = jax.ShapeDtypeStruct((arrived, hidden), F32)
    wide = pltpu.VMEM((devices * per, LANE), F32)
    narrow = pltpu.VMEM((arrived, half), BF16)
    params = pltpu.CompilerParams(vmem_limit_bytes=8 << 20)
    peer = swap(own)
    gate, up = pl.pallas_call(
        own_kernel,
        in_specs=[vmem_spec()] * 4,
        out_specs=[vmem_spec()] * 2,
        out_shape=[sums, sums],
        scratch_shapes=[wide, narrow],
        compiler_params=params,
        cost_estimate=estimate(4 * arrived * half * hidden, 4 * half * hidden),
    )(own, w_gate, w_up, w_down)
    act, send = pl.pallas_call(
        peer_kernel,
        in_specs=[vmem_spec()] * 6,
        out_specs=[vmem_spec()] * 2,
        out_shape=[jax.ShapeDtypeStruct((arrived, hidden), BF16), chunked],
        scratch_shapes=[wide, narrow],
        compiler_params=params,
        cost_estimate=estimate(6 * arrived * half * hidden, 6 * half * hidden),
    )(peer, gate, up, w_gate, w_up, w_down)
    received = swap(send)
    keep = pl.pallas_call(
        keep_kernel,
        in_specs=[vmem_spec()] * 2,
        out_specs=vmem_spec(),
        out_shape=chunked,
        scratch_shapes=[wide],
        compiler_params=params,
        cost_estimate=estimate(2 * arrived * half * hidden, 2 * half * hidden),
    )(act, w_down)
    return (keep.astype(F32) + received.astype(F32)).astype(BF16)


def combine_kernel(cap, weight_ref, back_ref, mixed_ref, a32_ref, attn_ref, out_ref, total32):
    rows, width = out_ref.shape
    total = width // LANE
    half = total // 2
    slots = weight_ref.shape[0] // rows
    for t in range(total):
        cols = slice(t * LANE, (t + 1) * LANE)
        attn_ref[:, cols] = a32_ref[pl.ds(t, rows, stride=total), :].astype(BF16)
    for c in range(2):
        acc = [
            mixed_ref[r * total + c * half : r * total + (c + 1) * half, :] for r in range(rows)
        ]
        for slot in range(slots):
            e, s = divmod(slot, cap)
            block = back_ref[2 * e + c, s * half : (s + 1) * half, :].astype(F32)
            for r in range(rows):
                acc[r] = acc[r] + weight_ref[r * slots + slot : r * slots + slot + 1, :] * block
        for r in range(rows):
            total32[r * total + c * half : r * total + (c + 1) * half, :] = acc[r]
    for t in range(total):
        out_ref[:, t * LANE : (t + 1) * LANE] = total32[pl.ds(t, rows, stride=total), :].astype(
            BF16
        )


def combine(weights, back, mixed, a32, rows, width, cap):
    shape = jax.ShapeDtypeStruct((rows, width), BF16)
    return pl.pallas_call(
        functools.partial(combine_kernel, cap),
        in_specs=[vmem_spec()] * 4,
        out_specs=[vmem_spec()] * 2,
        out_shape=[shape, shape],
        scratch_shapes=[pltpu.VMEM(mixed.shape, F32)],
        compiler_params=pltpu.CompilerParams(vmem_limit_bytes=6 << 20),
    )(weights, back, mixed, a32)


def body(
    hidden_in,
    queries,
    new_kv,
    kv_cache,
    lengths,
    w_out,
    w_gate,
    w_up,
    w_down,
    mlp_gain,
    expert_ids,
    route_weight,
):
    devices = lax.axis_size("node")
    rows, width = hidden_in.shape
    expert_count = devices // 2
    cap = max(2, -(-rows * expert_ids.shape[1] // expert_count))
    pairs = [(i, i ^ 1) for i in range(devices)]

    def swap(array):
        return lax.ppermute(array, "node", pairs)

    def exchange(array):
        return lax.all_to_all(array, "node", split_axis=0, concat_axis=0, tiled=True)

    gain = mlp_gain.reshape(width // LANE, LANE)
    context, weights, pick, h32, gain, w_keep = attention(
        queries,
        new_kv,
        kv_cache,
        lengths,
        expert_ids,
        route_weight,
        hidden_in,
        gain,
        w_out,
        devices,
        cap,
    )
    w_peer = swap(w_out)
    gathered = exchange(context)
    sums = exchange(project(gathered, w_keep, w_peer))
    a32, mixed, outgoing = norm_dispatch(sums, h32, gain, pick, cap)
    arrived = exchange(outgoing)
    back = exchange(experts(arrived, swap, w_gate, w_up, w_down, cap))
    return combine(weights, back, mixed, a32, rows, width, cap)


def solution(mesh):
    rows = P(("groups", "node"), None)
    return jax.shard_map(
        body,
        mesh=mesh,
        in_specs=(
            rows,
            rows,
            P(("groups", "node"), None, None),
            P(("groups", "node"), None, None, None),
            P(("groups", "node")),
            P("node", None),
            P("node", None, None),
            P("node", None, None),
            P("node", None, None),
            P(),
            rows,
            rows,
        ),
        out_specs=(rows, rows),
        check_vma=False,
    )
```

```python
import functools
import math

import jax
import jax.numpy as jnp
from jax import lax
from jax.experimental import pallas as pl
from jax.experimental.pallas import tpu as pltpu
from jax.sharding import PartitionSpec as P

HEAD = 128
LANE = 128
F32 = jnp.float32
BF16 = jnp.bfloat16


def vmem_spec():
    return pl.BlockSpec(memory_space=pltpu.VMEM)


def attention_kernel(
    cap,
    q_hbm,
    new_hbm,
    kv_hbm,
    len_hbm,
    ids_hbm,
    route_hbm,
    hidden_hbm,
    gain_hbm,
    w_hbm,
    out_ref,
    weight_ref,
    pick_ref,
    h32_ref,
    gain_ref,
    keep_ref,
    qv,
    nv,
    kv,
    hv,
    lens,
    ids,
    route,
    q32,
    ctx,
    count,
    sems,
):
    rows, heads, _ = ctx.shape
    slots = weight_ref.shape[0] // rows
    cache_len = kv.shape[2]
    kv_heads = kv.shape[3] // HEAD
    group = heads // kv_heads
    core = lax.axis_index("node") % 2
    half = w_hbm.shape[1] // 2
    mine = pl.ds(pl.multiple_of(core * half, half), half)
    pairs = [(ids_hbm, ids), (len_hbm, lens), (q_hbm, qv), (new_hbm, nv)]
    pairs += [(kv_hbm.at[r], kv.at[r]) for r in range(rows)]
    pairs += [(hidden_hbm, hv), (gain_hbm, gain_ref), (route_hbm, route)]
    pairs += [(w_hbm.at[:, mine], keep_ref)]
    copies = [
        pltpu.make_async_copy(source, target, sems.at[i])
        for i, (source, target) in enumerate(pairs)
    ]
    for copy in copies[: 7 + rows]:
        copy.start()
    copies[2].wait()
    for copy in copies[7 + rows :]:
        copy.start()
    for h in range(heads):
        q32[pl.ds(h, rows, stride=heads), :] = qv[:, h * HEAD : (h + 1) * HEAD].astype(F32)
    weight_ref[...] = jnp.zeros(weight_ref.shape, F32)
    pick_ref[...] = jnp.zeros(pick_ref.shape, F32)
    for e in range(slots // cap):
        count[e] = 0
    copies[0].wait()
    copies[6 + rows].wait()
    for row in range(rows):
        for k in range(ids.shape[1]):
            expert = ids[row, k]
            used = count[expert]
            count[expert] = used + 1
            slot = expert * cap + used
            weight_ref[pl.ds(row * slots + slot, 1), :] = jnp.full((1, LANE), route[row, k], F32)
            pick_ref[pl.ds(slot * rows + row, 1), :] = jnp.ones((1, LANE), F32)
    copies[1].wait()
    copies[3].wait()

    scale = 1.0 / math.sqrt(HEAD)
    spot = lax.broadcasted_iota(jnp.int32, (heads, cache_len), 1)
    batch = rows
    for start in range(0, rows, batch):
        chosen = range(start, start + batch)
        for r in chosen:
            copies[4 + r].wait()
        old, new, value, fresh = [], [], [], []
        for r in chosen:
            query = q32[r * heads : (r + 1) * heads, :]
            parts, fresh_key, fresh_value = [], [], []
            for g in range(kv_heads):
                cols = slice(g * HEAD, (g + 1) * HEAD)
                parts.append(
                    lax.dot_general(
                        query[g * group : (g + 1) * group].astype(BF16),
                        kv[r, 0, :, cols],
                        (((1,), (1,)), ((), ())),
                        preferred_element_type=F32,
                    )
                )
                fresh_key.append(jnp.broadcast_to(nv[r, 0:1, cols].astype(F32), (group, HEAD)))
                fresh_value.append(jnp.broadcast_to(nv[r, 1:2, cols].astype(F32), (group, HEAD)))
            scores = jnp.concatenate(parts, axis=0) * scale
            old.append(jnp.where(spot < lens[r], scores, -jnp.inf))
            new.append(
                jnp.sum(query * jnp.concatenate(fresh_key, axis=0), axis=1, keepdims=True) * scale
            )
            fresh.append(jnp.concatenate(fresh_value, axis=0))
        old = jnp.concatenate(old, axis=0)
        new = jnp.concatenate(new, axis=0)
        top = jnp.maximum(jnp.max(old, axis=1, keepdims=True), new)
        old = jnp.exp(old - top)
        new = jnp.exp(new - top)
        share = 1.0 / (jnp.sum(old, axis=1, keepdims=True) + new)
        probs = (old * share).astype(BF16)
        new = (new * share).astype(BF16).astype(F32)
        for i, r in enumerate(chosen):
            for g in range(kv_heads):
                first = i * heads + g * group
                value.append(
                    jnp.dot(
                        probs[first : first + group],
                        kv[r, 1, :, g * HEAD : (g + 1) * HEAD],
                        preferred_element_type=F32,
                    )
                )
        result = jnp.concatenate(value, axis=0) + new * jnp.concatenate(fresh, axis=0)
        for i, r in enumerate(chosen):
            ctx[r] = result[i * heads : (i + 1) * heads]

    chips = out_ref.shape[0] // 2
    each = heads // chips
    for i in range(chips):
        block = jnp.concatenate(
            [ctx[r, i * each : (i + 1) * each, :] for r in range(rows)], axis=0
        ).astype(BF16)
        out_ref[2 * i] = block
        out_ref[2 * i + 1] = block
    copies[4 + rows].wait()
    total = h32_ref.shape[0] // rows
    for t in range(total):
        cols = slice(t * LANE, (t + 1) * LANE)
        h32_ref[pl.ds(t, rows, stride=total), :] = hv[:, cols].astype(F32)
    copies[5 + rows].wait()
    for copy in copies[7 + rows :]:
        copy.wait()


def attention(
    queries, new_kv, kv_cache, lengths, expert_ids, route_weight, hidden_in, gain, w_out, devices, cap
):
    rows, width = hidden_in.shape
    heads = queries.shape[1] // HEAD
    each = heads // (devices // 2)
    experts = devices // 2
    half = jax.ShapeDtypeStruct((w_out.shape[0], width // 2), BF16)
    table = jax.ShapeDtypeStruct((rows * experts * cap, LANE), F32)
    arrays = (
        queries,
        new_kv,
        kv_cache,
        lengths,
        expert_ids,
        route_weight,
        hidden_in,
        gain,
        w_out,
    )
    return pl.pallas_call(
        functools.partial(attention_kernel, cap),
        in_specs=[pl.BlockSpec(memory_space=pltpu.HBM)] * len(arrays),
        out_specs=[vmem_spec()] * 6,
        out_shape=[
            jax.ShapeDtypeStruct((devices, rows * each, LANE), BF16),
            table,
            table,
            jax.ShapeDtypeStruct((rows * width // LANE, LANE), F32),
            jax.ShapeDtypeStruct(gain.shape, F32),
            half,
        ],
        scratch_shapes=[
            pltpu.VMEM(queries.shape, BF16),
            pltpu.VMEM(new_kv.shape, BF16),
            pltpu.VMEM(kv_cache.shape, BF16),
            pltpu.VMEM(hidden_in.shape, BF16),
            pltpu.SMEM(lengths.shape, jnp.int32),
            pltpu.SMEM(expert_ids.shape, jnp.int32),
            pltpu.SMEM(route_weight.shape, F32),
            pltpu.VMEM((rows * heads, LANE), F32),
            pltpu.VMEM((rows, heads, LANE), F32),
            pltpu.SMEM((experts,), jnp.int32),
            pltpu.SemaphoreType.DMA((8 + rows,)),
        ],
        compiler_params=pltpu.CompilerParams(vmem_limit_bytes=12 << 20),
    )(*(pltpu.with_memory_space_constraint(array, pltpu.HBM) for array in arrays))


def project_kernel(ctx_ref, own_ref, peer_ref, out_ref, x32, o32):
    devices, per, _ = ctx_ref.shape
    x32[...] = ctx_ref[...].reshape(devices * per, LANE).astype(F32)
    core = lax.axis_index("node") % 2
    held, width = own_ref.shape
    each = 2 * held // LANE
    chunks = width // LANE
    sums = o32.shape[0] // chunks

    def left(first):
        return jnp.concatenate(
            [
                x32[pl.ds(first + j, sums, stride=each), :].astype(BF16)
                for j in range(held // LANE)
            ],
            axis=1,
        )

    def half_cols(first, step):
        return pl.ds(pl.multiple_of(core * width + first, LANE), step)

    own_left = left(core * (held // LANE))
    peer_left = left((1 - core) * (held // LANE))
    step = 512
    for first in range(0, width, step):
        cols = slice(first, first + step)
        total = jnp.dot(own_left, own_ref[:, cols], preferred_element_type=F32) + jnp.dot(
            peer_left, peer_ref[:, half_cols(first, step)], preferred_element_type=F32
        )
        for t in range(step // LANE):
            o32[pl.ds(first // LANE + t, sums, stride=chunks), :] = total[
                :, t * LANE : (t + 1) * LANE
            ]
    sides = o32[...].reshape(2, devices // 2, o32.shape[0] // devices, LANE).astype(BF16)
    for side in range(2):
        out_ref[:, side] = sides[side]


def project(gathered, w_own, w_peer):
    devices, per, _ = gathered.shape
    held, width = w_own.shape
    rows = per // (2 * held // LANE)
    chunks = width // LANE
    return pl.pallas_call(
        project_kernel,
        in_specs=[vmem_spec()] * 3,
        out_specs=vmem_spec(),
        out_shape=jax.ShapeDtypeStruct((devices // 2, 2, rows * chunks, LANE), BF16),
        scratch_shapes=[
            pltpu.VMEM((devices * per, LANE), F32),
            pltpu.VMEM((devices * rows * chunks, LANE), F32),
        ],
        compiler_params=pltpu.CompilerParams(vmem_limit_bytes=12 << 20),
    )(gathered, w_own, w_peer)


def my_side():
    return lax.axis_index("node") // (lax.axis_size("node") // 2)


def share_kernel(sums_ref, h32_ref, pick_ref, part_ref, pay_ref):
    devices, _, per, _ = sums_ref.shape
    size = h32_ref.shape[0]
    rows = pick_ref.shape[0] // (pay_ref.shape[0] - 2 * size) // 2
    total = size // rows
    half = total // 2
    side = my_side()
    for c in range(2):
        for h in range(2):
            acc = sums_ref[c, h].astype(F32)
            for k in range(1, devices // 2):
                acc = acc + sums_ref[2 * k + c, h].astype(F32)
            for r in range(rows):
                first = r * total + c * half
                part_ref[h, first : first + half, :] = acc[r * half : (r + 1) * half]
    pay_ref[:size] = part_ref[1 - side].astype(BF16)
    pay_ref[size : 2 * size] = (part_ref[side] + h32_ref[...]).astype(BF16)
    slots = pay_ref.shape[0] - 2 * size
    lane = lax.broadcasted_iota(jnp.int32, (slots, LANE), 1)
    tile = jnp.zeros((slots, LANE), F32)
    for r in range(rows):
        chosen = pick_ref[pl.ds((1 - side) * slots * rows + r, slots, stride=rows), :]
        tile = jnp.where(lane // (LANE // rows) == r, chosen, tile)
    pay_ref[2 * size :] = tile.astype(BF16)


def share(sums, h32, pick, slots):
    size = h32.shape[0]
    return pl.pallas_call(
        share_kernel,
        in_specs=[vmem_spec()] * 3,
        out_specs=[vmem_spec()] * 2,
        out_shape=[
            jax.ShapeDtypeStruct((2, size, LANE), F32),
            jax.ShapeDtypeStruct((2 * size + slots, LANE), BF16),
        ],
        compiler_params=pltpu.CompilerParams(vmem_limit_bytes=6 << 20),
    )(sums, h32, pick)


def norm_kernel(
    cap, part_ref, pay_ref, h32_ref, gain_ref, pick_ref, attn_ref, mixed_ref, out_ref
):
    total = gain_ref.shape[0]
    size = h32_ref.shape[0]
    rows = size // total
    half = total // 2
    slots = pay_ref.shape[0] - 2 * size
    side = my_side()
    attn = part_ref[side] + pay_ref[:size].astype(F32)
    attn_ref[...] = attn
    own = h32_ref[...] + attn.astype(BF16).astype(F32)
    mixed_ref[...] = own
    mirror = part_ref[1 - side] + pay_ref[size : 2 * size].astype(F32)

    def normed(state):
        result = []
        for r in range(rows):
            mixed = state[r * total : (r + 1) * total]
            square = jnp.sum(jnp.sum(mixed * mixed, axis=0, keepdims=True), axis=1, keepdims=True)
            result.append(mixed * lax.rsqrt(square / width_of(total) + 1e-06) * gain_ref[...])
        return result

    tile = pay_ref[2 * size :].astype(F32)
    lane = lax.broadcasted_iota(jnp.int32, (slots, LANE), 1)
    taken = [
        jnp.max(jnp.where(lane // (LANE // rows) == r, tile, 0.0), axis=1, keepdims=True)
        for r in range(rows)
    ]
    first = side * slots * rows
    kept = [pick_ref[pl.ds(first + r, slots, stride=rows), :] for r in range(rows)]
    for state, picks, where in ((own, kept, side), (mirror, taken, 1 - side)):
        lines = normed(state)
        for slot in range(slots):
            chosen = lines[0] * picks[0][slot : slot + 1, :]
            for r in range(1, rows):
                chosen = chosen + lines[r] * picks[r][slot : slot + 1, :]
            chosen = chosen.astype(BF16)
            e, s = divmod(slot, cap)
            for c in range(2):
                out_ref[2 * e + c, where, s * half : (s + 1) * half, :] = chosen[
                    c * half : (c + 1) * half
                ]


def width_of(chunks):
    return chunks * LANE


def norm_dispatch(part, pay, h32, gain, pick, devices, cap):
    total = gain.shape[0]
    state = jax.ShapeDtypeStruct(h32.shape, F32)
    return pl.pallas_call(
        functools.partial(norm_kernel, cap),
        in_specs=[vmem_spec()] * 5,
        out_specs=[vmem_spec()] * 3,
        out_shape=[
            state,
            state,
            jax.ShapeDtypeStruct((devices // 2, 2, cap * total // 2, LANE), BF16),
        ],
        compiler_params=pltpu.CompilerParams(vmem_limit_bytes=6 << 20),
    )(part, pay, h32, gain, pick)


def rows_from_chunks(ref, x32, x16):
    devices, per, _ = ref.shape
    arrived, width = x16.shape
    half = width // LANE
    x32[...] = ref[...].reshape(devices * per, LANE).astype(F32)
    for t in range(half):
        x16[:, t * LANE : (t + 1) * LANE] = x32[pl.ds(t, arrived, stride=half), :].astype(BF16)


def chunks_from_rows(result, x32, ref):
    arrived, width = result.shape
    half = width // LANE
    for t in range(half):
        x32[pl.ds(t, arrived, stride=half), :] = result[:, t * LANE : (t + 1) * LANE]
    devices, per, _ = ref.shape
    blocks = x32[...].reshape(devices // 2, 2, per, LANE).astype(BF16)
    for side in range(2):
        ref[side * (devices // 2) : (side + 1) * (devices // 2)] = blocks[:, side]


def half_of(which, size):
    return pl.ds(pl.multiple_of(which * size, size), size)


def own_kernel(own_ref, gate_ref, up_ref, down_ref, gate_out, up_out, x32, x16):
    rows_from_chunks(own_ref, x32, x16)
    span = half_of(lax.axis_index("node") % 2, x16.shape[1])
    gate_out[...] = jnp.dot(x16[...], gate_ref[0, span, :], preferred_element_type=F32)
    up_out[...] = jnp.dot(x16[...], up_ref[0, span, :], preferred_element_type=F32)


def peer_kernel(
    peer_ref, gate_in, up_in, gate_ref, up_ref, down_ref, act_ref, send_ref, x32, x16
):
    rows_from_chunks(peer_ref, x32, x16)
    span = half_of(1 - lax.axis_index("node") % 2, x16.shape[1])
    gate = gate_in[...] + jnp.dot(x16[...], gate_ref[0, span, :], preferred_element_type=F32)
    up = up_in[...] + jnp.dot(x16[...], up_ref[0, span, :], preferred_element_type=F32)
    act = (gate / (1.0 + jnp.exp(-gate)) * up).astype(BF16)
    act_ref[...] = act
    result = jnp.dot(act, down_ref[0, :, span], preferred_element_type=F32)
    chunks_from_rows(result, x32, send_ref)


def keep_kernel(act_ref, down_ref, keep_ref, x32):
    size = down_ref.shape[2] // 2
    span = half_of(lax.axis_index("node") % 2, size)
    result = jnp.dot(act_ref[...], down_ref[0, :, span], preferred_element_type=F32)
    chunks_from_rows(result, x32, keep_ref)


def estimate(flops, moved):
    return pl.CostEstimate(flops=flops, bytes_accessed=moved, transcendentals=0)


def experts(own, swap, w_gate, w_up, w_down, cap):
    devices, per, _ = own.shape
    half = per // (2 * cap) * LANE
    arrived = devices * 2 * cap
    hidden = w_gate.shape[2]
    chunked = jax.ShapeDtypeStruct((2 * devices, per // 2, LANE), BF16)
    sums = jax.ShapeDtypeStruct((arrived, hidden), F32)
    wide = pltpu.VMEM((devices * per, LANE), F32)
    narrow = pltpu.VMEM((arrived, half), BF16)
    params = pltpu.CompilerParams(vmem_limit_bytes=8 << 20)
    peer = swap(own)
    gate, up = pl.pallas_call(
        own_kernel,
        in_specs=[vmem_spec()] * 4,
        out_specs=[vmem_spec()] * 2,
        out_shape=[sums, sums],
        scratch_shapes=[wide, narrow],
        compiler_params=params,
        cost_estimate=estimate(4 * arrived * half * hidden, 4 * half * hidden),
    )(own, w_gate, w_up, w_down)
    act, send = pl.pallas_call(
        peer_kernel,
        in_specs=[vmem_spec()] * 6,
        out_specs=[vmem_spec()] * 2,
        out_shape=[jax.ShapeDtypeStruct((arrived, hidden), BF16), chunked],
        scratch_shapes=[wide, narrow],
        compiler_params=params,
        cost_estimate=estimate(6 * arrived * half * hidden, 6 * half * hidden),
    )(peer, gate, up, w_gate, w_up, w_down)
    received = swap(send)
    keep = pl.pallas_call(
        keep_kernel,
        in_specs=[vmem_spec()] * 2,
        out_specs=vmem_spec(),
        out_shape=chunked,
        scratch_shapes=[wide],
        compiler_params=params,
        cost_estimate=estimate(2 * arrived * half * hidden, 2 * half * hidden),
    )(act, w_down)
    return (keep.astype(F32) + received.astype(F32)).astype(BF16)


def combine_kernel(cap, weight_ref, back_ref, mixed_ref, a32_ref, attn_ref, out_ref, total32):
    rows, width = out_ref.shape
    total = width // LANE
    half = total // 2
    slots = weight_ref.shape[0] // rows
    for t in range(total):
        cols = slice(t * LANE, (t + 1) * LANE)
        attn_ref[:, cols] = a32_ref[pl.ds(t, rows, stride=total), :].astype(BF16)
    for c in range(2):
        acc = [
            mixed_ref[r * total + c * half : r * total + (c + 1) * half, :] for r in range(rows)
        ]
        for slot in range(slots):
            e, s = divmod(slot, cap)
            block = back_ref[2 * e + c, s * half : (s + 1) * half, :].astype(F32)
            for r in range(rows):
                acc[r] = acc[r] + weight_ref[r * slots + slot : r * slots + slot + 1, :] * block
        for r in range(rows):
            total32[r * total + c * half : r * total + (c + 1) * half, :] = acc[r]
    for t in range(total):
        out_ref[:, t * LANE : (t + 1) * LANE] = total32[pl.ds(t, rows, stride=total), :].astype(
            BF16
        )


def combine(weights, back, mixed, a32, rows, width, cap):
    shape = jax.ShapeDtypeStruct((rows, width), BF16)
    return pl.pallas_call(
        functools.partial(combine_kernel, cap),
        in_specs=[vmem_spec()] * 4,
        out_specs=[vmem_spec()] * 2,
        out_shape=[shape, shape],
        scratch_shapes=[pltpu.VMEM(mixed.shape, F32)],
        compiler_params=pltpu.CompilerParams(vmem_limit_bytes=6 << 20),
    )(weights, back, mixed, a32)


def body(
    hidden_in,
    queries,
    new_kv,
    kv_cache,
    lengths,
    w_out,
    w_gate,
    w_up,
    w_down,
    mlp_gain,
    expert_ids,
    route_weight,
):
    devices = lax.axis_size("node")
    rows, width = hidden_in.shape
    expert_count = devices // 2
    cap = max(2, -(-rows * expert_ids.shape[1] // expert_count))
    pairs = [(i, i ^ 1) for i in range(devices)]

    def swap(array):
        return lax.ppermute(array, "node", pairs)

    def exchange(array):
        return lax.all_to_all(array, "node", split_axis=0, concat_axis=0, tiled=True)

    side = devices // 2
    sides = [list(range(side)), list(range(side, devices))]

    def exchange_inside(array):
        return lax.all_to_all(
            array, "node", split_axis=0, concat_axis=0, tiled=True, axis_index_groups=sides
        )

    gain = mlp_gain.reshape(width // LANE, LANE)
    context, weights, pick, h32, gain, w_keep = attention(
        queries,
        new_kv,
        kv_cache,
        lengths,
        expert_ids,
        route_weight,
        hidden_in,
        gain,
        w_out,
        devices,
        cap,
    )
    w_peer = swap(w_out)
    gathered = exchange(context)
    sums = exchange_inside(project(gathered, w_keep, w_peer))
    part, pay = share(sums, h32, pick, expert_count // 2 * cap)
    pay = lax.ppermute(pay, "node", [(i, i ^ side) for i in range(devices)])
    a32, mixed, outgoing = norm_dispatch(part, pay, h32, gain, pick, devices, cap)
    arrived = exchange_inside(outgoing)
    arrived = arrived.reshape(side, -1, LANE)
    back = exchange(experts(arrived, swap, w_gate, w_up, w_down, cap))
    return combine(weights, back, mixed, a32, rows, width, cap)


def solution(mesh):
    rows = P(("groups", "node"), None)
    return jax.shard_map(
        body,
        mesh=mesh,
        in_specs=(
            rows,
            rows,
            P(("groups", "node"), None, None),
            P(("groups", "node"), None, None, None),
            P(("groups", "node")),
            P("node", None),
            P("node", None, None),
            P("node", None, None),
            P("node", None, None),
            P(),
            rows,
            rows,
        ),
        out_specs=(rows, rows),
        check_vma=False,
    )
```

```python
import functools
import math

import jax
import jax.numpy as jnp
from jax import lax
from jax.experimental import pallas as pl
from jax.experimental.pallas import tpu as pltpu
from jax.sharding import PartitionSpec as P

HEAD = 128
LANE = 128
F32 = jnp.float32
BF16 = jnp.bfloat16


def vmem_spec():
    return pl.BlockSpec(memory_space=pltpu.VMEM)


def attention_kernel(
    cap,
    q_hbm,
    new_hbm,
    kv_hbm,
    len_hbm,
    ids_hbm,
    route_hbm,
    hidden_hbm,
    gain_hbm,
    w_hbm,
    out_ref,
    weight_ref,
    pick_ref,
    h32_ref,
    gain_ref,
    keep_ref,
    qv,
    nv,
    kv,
    hv,
    lens,
    ids,
    route,
    q32,
    ctx,
    count,
    sems,
):
    rows, heads, _ = ctx.shape
    slots = weight_ref.shape[0] // rows
    cache_len = kv.shape[2]
    kv_heads = kv.shape[3] // HEAD
    group = heads // kv_heads
    core = lax.axis_index("node") % 2
    half = w_hbm.shape[1] // 2
    mine = pl.ds(pl.multiple_of(core * half, half), half)
    pairs = [(ids_hbm, ids), (len_hbm, lens), (q_hbm, qv), (new_hbm, nv)]
    pairs += [(kv_hbm.at[r], kv.at[r]) for r in range(rows)]
    pairs += [(hidden_hbm, hv), (gain_hbm, gain_ref), (route_hbm, route)]
    pairs += [(w_hbm.at[:, mine], keep_ref)]
    copies = [
        pltpu.make_async_copy(source, target, sems.at[i])
        for i, (source, target) in enumerate(pairs)
    ]
    for copy in copies[: 7 + rows]:
        copy.start()
    copies[2].wait()
    for copy in copies[7 + rows :]:
        copy.start()
    for h in range(heads):
        q32[pl.ds(h, rows, stride=heads), :] = qv[:, h * HEAD : (h + 1) * HEAD].astype(F32)
    weight_ref[...] = jnp.zeros(weight_ref.shape, F32)
    pick_ref[...] = jnp.zeros(pick_ref.shape, F32)
    for e in range(slots // cap):
        count[e] = 0
    copies[0].wait()
    copies[6 + rows].wait()
    for row in range(rows):
        for k in range(ids.shape[1]):
            expert = ids[row, k]
            used = count[expert]
            count[expert] = used + 1
            slot = expert * cap + used
            weight_ref[pl.ds(row * slots + slot, 1), :] = jnp.full((1, LANE), route[row, k], F32)
            pick_ref[pl.ds(slot * rows + row, 1), :] = jnp.ones((1, LANE), F32)
    copies[1].wait()
    copies[3].wait()

    scale = 1.0 / math.sqrt(HEAD)
    spot = lax.broadcasted_iota(jnp.int32, (heads, cache_len), 1)
    batch = rows
    for start in range(0, rows, batch):
        chosen = range(start, start + batch)
        for r in chosen:
            copies[4 + r].wait()
        old, new, value, fresh = [], [], [], []
        for r in chosen:
            query = q32[r * heads : (r + 1) * heads, :]
            parts, fresh_key, fresh_value = [], [], []
            for g in range(kv_heads):
                cols = slice(g * HEAD, (g + 1) * HEAD)
                parts.append(
                    lax.dot_general(
                        query[g * group : (g + 1) * group].astype(BF16),
                        kv[r, 0, :, cols],
                        (((1,), (1,)), ((), ())),
                        preferred_element_type=F32,
                    )
                )
                fresh_key.append(jnp.broadcast_to(nv[r, 0:1, cols].astype(F32), (group, HEAD)))
                fresh_value.append(jnp.broadcast_to(nv[r, 1:2, cols].astype(F32), (group, HEAD)))
            scores = jnp.concatenate(parts, axis=0) * scale
            old.append(jnp.where(spot < lens[r], scores, -jnp.inf))
            new.append(
                jnp.sum(query * jnp.concatenate(fresh_key, axis=0), axis=1, keepdims=True) * scale
            )
            fresh.append(jnp.concatenate(fresh_value, axis=0))
        old = jnp.concatenate(old, axis=0)
        new = jnp.concatenate(new, axis=0)
        top = jnp.maximum(jnp.max(old, axis=1, keepdims=True), new)
        old = jnp.exp(old - top)
        new = jnp.exp(new - top)
        share = 1.0 / (jnp.sum(old, axis=1, keepdims=True) + new)
        probs = (old * share).astype(BF16)
        new = (new * share).astype(BF16).astype(F32)
        for i, r in enumerate(chosen):
            for g in range(kv_heads):
                first = i * heads + g * group
                value.append(
                    jnp.dot(
                        probs[first : first + group],
                        kv[r, 1, :, g * HEAD : (g + 1) * HEAD],
                        preferred_element_type=F32,
                    )
                )
        result = jnp.concatenate(value, axis=0) + new * jnp.concatenate(fresh, axis=0)
        for i, r in enumerate(chosen):
            ctx[r] = result[i * heads : (i + 1) * heads]

    chips = out_ref.shape[0] // 2
    each = heads // chips
    for i in range(chips):
        block = jnp.concatenate(
            [ctx[r, i * each : (i + 1) * each, :] for r in range(rows)], axis=0
        ).astype(BF16)
        out_ref[2 * i] = block
        out_ref[2 * i + 1] = block
    copies[4 + rows].wait()
    total = h32_ref.shape[0] // rows
    for t in range(total):
        cols = slice(t * LANE, (t + 1) * LANE)
        h32_ref[pl.ds(t, rows, stride=total), :] = hv[:, cols].astype(F32)
    copies[5 + rows].wait()
    for copy in copies[7 + rows :]:
        copy.wait()


def attention(
    queries, new_kv, kv_cache, lengths, expert_ids, route_weight, hidden_in, gain, w_out, devices, cap
):
    rows, width = hidden_in.shape
    heads = queries.shape[1] // HEAD
    each = heads // (devices // 2)
    experts = devices // 2
    half = jax.ShapeDtypeStruct((w_out.shape[0], width // 2), BF16)
    table = jax.ShapeDtypeStruct((rows * experts * cap, LANE), F32)
    arrays = (
        queries,
        new_kv,
        kv_cache,
        lengths,
        expert_ids,
        route_weight,
        hidden_in,
        gain,
        w_out,
    )
    return pl.pallas_call(
        functools.partial(attention_kernel, cap),
        in_specs=[pl.BlockSpec(memory_space=pltpu.HBM)] * len(arrays),
        out_specs=[vmem_spec()] * 6,
        out_shape=[
            jax.ShapeDtypeStruct((devices, rows * each, LANE), BF16),
            table,
            table,
            jax.ShapeDtypeStruct((rows * width // LANE, LANE), F32),
            jax.ShapeDtypeStruct(gain.shape, F32),
            half,
        ],
        scratch_shapes=[
            pltpu.VMEM(queries.shape, BF16),
            pltpu.VMEM(new_kv.shape, BF16),
            pltpu.VMEM(kv_cache.shape, BF16),
            pltpu.VMEM(hidden_in.shape, BF16),
            pltpu.SMEM(lengths.shape, jnp.int32),
            pltpu.SMEM(expert_ids.shape, jnp.int32),
            pltpu.SMEM(route_weight.shape, F32),
            pltpu.VMEM((rows * heads, LANE), F32),
            pltpu.VMEM((rows, heads, LANE), F32),
            pltpu.SMEM((experts,), jnp.int32),
            pltpu.SemaphoreType.DMA((8 + rows,)),
        ],
        compiler_params=pltpu.CompilerParams(vmem_limit_bytes=12 << 20),
    )(*(pltpu.with_memory_space_constraint(array, pltpu.HBM) for array in arrays))


def project_kernel(ctx_ref, own_ref, peer_ref, out_ref, x32, o32):
    devices, per, _ = ctx_ref.shape
    x32[...] = ctx_ref[...].reshape(devices * per, LANE).astype(F32)
    core = lax.axis_index("node") % 2
    held, width = own_ref.shape
    each = 2 * held // LANE
    chunks = width // LANE
    sums = o32.shape[0] // chunks

    def left(first):
        return jnp.concatenate(
            [
                x32[pl.ds(first + j, sums, stride=each), :].astype(BF16)
                for j in range(held // LANE)
            ],
            axis=1,
        )

    def half_cols(first, step):
        return pl.ds(pl.multiple_of(core * width + first, LANE), step)

    own_left = left(core * (held // LANE))
    peer_left = left((1 - core) * (held // LANE))
    step = 512
    for first in range(0, width, step):
        cols = slice(first, first + step)
        total = jnp.dot(own_left, own_ref[:, cols], preferred_element_type=F32) + jnp.dot(
            peer_left, peer_ref[:, half_cols(first, step)], preferred_element_type=F32
        )
        for t in range(step // LANE):
            o32[pl.ds(first // LANE + t, sums, stride=chunks), :] = total[
                :, t * LANE : (t + 1) * LANE
            ]
    sides = o32[...].reshape(2, devices // 2, o32.shape[0] // devices, LANE).astype(BF16)
    for side in range(2):
        out_ref[:, side] = sides[side]


def project(gathered, w_own, w_peer):
    devices, per, _ = gathered.shape
    held, width = w_own.shape
    rows = per // (2 * held // LANE)
    chunks = width // LANE
    return pl.pallas_call(
        project_kernel,
        in_specs=[vmem_spec()] * 3,
        out_specs=vmem_spec(),
        out_shape=jax.ShapeDtypeStruct((devices // 2, 2, rows * chunks, LANE), BF16),
        scratch_shapes=[
            pltpu.VMEM((devices * per, LANE), F32),
            pltpu.VMEM((devices * rows * chunks, LANE), F32),
        ],
        compiler_params=pltpu.CompilerParams(vmem_limit_bytes=12 << 20),
    )(gathered, w_own, w_peer)


def my_side():
    return lax.axis_index("node") // (lax.axis_size("node") // 2)


def share_kernel(sums_ref, h32_ref, pick_ref, part_ref, pay_ref):
    devices, _, per, _ = sums_ref.shape
    size = h32_ref.shape[0]
    rows = pick_ref.shape[0] // (pay_ref.shape[0] - 2 * size) // 2
    total = size // rows
    half = total // 2
    side = my_side()
    for c in range(2):
        for h in range(2):
            acc = sums_ref[c, h].astype(F32)
            for k in range(1, devices // 2):
                acc = acc + sums_ref[2 * k + c, h].astype(F32)
            for r in range(rows):
                first = r * total + c * half
                part_ref[h, first : first + half, :] = acc[r * half : (r + 1) * half]
    pay_ref[:size] = part_ref[1 - side].astype(BF16)
    pay_ref[size : 2 * size] = (part_ref[side] + h32_ref[...]).astype(BF16)
    slots = pay_ref.shape[0] - 2 * size
    lane = lax.broadcasted_iota(jnp.int32, (slots, LANE), 1)
    tile = jnp.zeros((slots, LANE), F32)
    for r in range(rows):
        chosen = pick_ref[pl.ds((1 - side) * slots * rows + r, slots, stride=rows), :]
        tile = jnp.where(lane // (LANE // rows) == r, chosen, tile)
    pay_ref[2 * size :] = tile.astype(BF16)


def share(sums, h32, pick, slots):
    size = h32.shape[0]
    return pl.pallas_call(
        share_kernel,
        in_specs=[vmem_spec()] * 3,
        out_specs=[vmem_spec()] * 2,
        out_shape=[
            jax.ShapeDtypeStruct((2, size, LANE), F32),
            jax.ShapeDtypeStruct((2 * size + slots, LANE), BF16),
        ],
        compiler_params=pltpu.CompilerParams(vmem_limit_bytes=6 << 20),
    )(sums, h32, pick)


def norm_kernel(
    cap, part_ref, pay_ref, h32_ref, gain_ref, pick_ref, down_ref, attn_ref, mixed_ref, out_ref
):
    total = gain_ref.shape[0]
    size = h32_ref.shape[0]
    rows = size // total
    half = total // 2
    slots = pay_ref.shape[0] - 2 * size
    side = my_side()
    attn = part_ref[side] + pay_ref[:size].astype(F32)
    attn_ref[...] = attn
    own = h32_ref[...] + attn.astype(BF16).astype(F32)
    mixed_ref[...] = own
    mirror = part_ref[1 - side] + pay_ref[size : 2 * size].astype(F32)

    def normed(state):
        result = []
        for r in range(rows):
            mixed = state[r * total : (r + 1) * total]
            square = jnp.sum(jnp.sum(mixed * mixed, axis=0, keepdims=True), axis=1, keepdims=True)
            result.append(mixed * lax.rsqrt(square / width_of(total) + 1e-06) * gain_ref[...])
        return result

    tile = pay_ref[2 * size :].astype(F32)
    lane = lax.broadcasted_iota(jnp.int32, (slots, LANE), 1)
    taken = [
        jnp.max(jnp.where(lane // (LANE // rows) == r, tile, 0.0), axis=1, keepdims=True)
        for r in range(rows)
    ]
    first = side * slots * rows
    kept = [pick_ref[pl.ds(first + r, slots, stride=rows), :] for r in range(rows)]
    for state, picks, where in ((own, kept, side), (mirror, taken, 1 - side)):
        lines = normed(state)
        for slot in range(slots):
            chosen = lines[0] * picks[0][slot : slot + 1, :]
            for r in range(1, rows):
                chosen = chosen + lines[r] * picks[r][slot : slot + 1, :]
            chosen = chosen.astype(BF16)
            e, s = divmod(slot, cap)
            for c in range(2):
                out_ref[2 * e + c, where, s * half : (s + 1) * half, :] = chosen[
                    c * half : (c + 1) * half
                ]


def width_of(chunks):
    return chunks * LANE


def norm_dispatch(part, pay, h32, gain, pick, w_down, devices, cap):
    total = gain.shape[0]
    state = jax.ShapeDtypeStruct(h32.shape, F32)
    return pl.pallas_call(
        functools.partial(norm_kernel, cap),
        in_specs=[vmem_spec()] * 6,
        out_specs=[vmem_spec()] * 3,
        out_shape=[
            state,
            state,
            jax.ShapeDtypeStruct((devices // 2, 2, cap * total // 2, LANE), BF16),
        ],
        compiler_params=pltpu.CompilerParams(vmem_limit_bytes=6 << 20),
    )(part, pay, h32, gain, pick, w_down)


def rows_from_chunks(ref, x32, x16):
    devices, per, _ = ref.shape
    arrived, width = x16.shape
    half = width // LANE
    x32[...] = ref[...].reshape(devices * per, LANE).astype(F32)
    for t in range(half):
        x16[:, t * LANE : (t + 1) * LANE] = x32[pl.ds(t, arrived, stride=half), :].astype(BF16)


def chunks_from_rows(result, x32, ref):
    arrived, width = result.shape
    half = width // LANE
    for t in range(half):
        x32[pl.ds(t, arrived, stride=half), :] = result[:, t * LANE : (t + 1) * LANE]
    devices, per, _ = ref.shape
    blocks = x32[...].reshape(devices // 2, 2, per, LANE).astype(BF16)
    for side in range(2):
        ref[side * (devices // 2) : (side + 1) * (devices // 2)] = blocks[:, side]


def half_of(which, size):
    return pl.ds(pl.multiple_of(which * size, size), size)


def own_kernel(own_ref, gate_ref, up_ref, gate_out, up_out, x32, x16):
    rows_from_chunks(own_ref, x32, x16)
    span = half_of(lax.axis_index("node") % 2, x16.shape[1])
    gate_out[...] = jnp.dot(x16[...], gate_ref[0, span, :], preferred_element_type=F32)
    up_out[...] = jnp.dot(x16[...], up_ref[0, span, :], preferred_element_type=F32)


def peer_kernel(
    peer_ref, gate_in, up_in, gate_ref, up_ref, down_ref, act_ref, send_ref, x32, x16
):
    rows_from_chunks(peer_ref, x32, x16)
    span = half_of(1 - lax.axis_index("node") % 2, x16.shape[1])
    gate = gate_in[...] + jnp.dot(x16[...], gate_ref[0, span, :], preferred_element_type=F32)
    up = up_in[...] + jnp.dot(x16[...], up_ref[0, span, :], preferred_element_type=F32)
    act = (gate / (1.0 + jnp.exp(-gate)) * up).astype(BF16)
    act_ref[...] = act
    result = jnp.dot(act, down_ref[0, :, span], preferred_element_type=F32)
    chunks_from_rows(result, x32, send_ref)


def keep_kernel(act_ref, down_ref, a32_ref, keep_ref, attn_hbm, x32, attn, sem):
    rows, width = attn.shape
    total = width // LANE
    for t in range(total):
        attn[:, t * LANE : (t + 1) * LANE] = a32_ref[pl.ds(t, rows, stride=total), :].astype(BF16)
    copy = pltpu.make_async_copy(attn, attn_hbm, sem)
    copy.start()
    size = down_ref.shape[2] // 2
    span = half_of(lax.axis_index("node") % 2, size)
    result = jnp.dot(act_ref[...], down_ref[0, :, span], preferred_element_type=F32)
    chunks_from_rows(result, x32, keep_ref)
    copy.wait()


def estimate(flops, moved):
    return pl.CostEstimate(flops=flops, bytes_accessed=moved, transcendentals=0)


def experts(own, swap, w_gate, w_up, w_down, a32, cap):
    devices, per, _ = own.shape
    half = per // (2 * cap) * LANE
    arrived = devices * 2 * cap
    hidden = w_gate.shape[2]
    chunked = jax.ShapeDtypeStruct((2 * devices, per // 2, LANE), BF16)
    sums = jax.ShapeDtypeStruct((arrived, hidden), F32)
    wide = pltpu.VMEM((devices * per, LANE), F32)
    narrow = pltpu.VMEM((arrived, half), BF16)
    params = pltpu.CompilerParams(vmem_limit_bytes=8 << 20)
    peer = swap(own)
    gate, up = pl.pallas_call(
        own_kernel,
        in_specs=[vmem_spec()] * 3,
        out_specs=[vmem_spec()] * 2,
        out_shape=[sums, sums],
        scratch_shapes=[wide, narrow],
        compiler_params=params,
        cost_estimate=estimate(4 * arrived * half * hidden, 4 * half * hidden),
    )(own, w_gate, w_up)
    act, send = pl.pallas_call(
        peer_kernel,
        in_specs=[vmem_spec()] * 6,
        out_specs=[vmem_spec()] * 2,
        out_shape=[jax.ShapeDtypeStruct((arrived, hidden), BF16), chunked],
        scratch_shapes=[wide, narrow],
        compiler_params=params,
        cost_estimate=estimate(6 * arrived * half * hidden, 6 * half * hidden),
    )(peer, gate, up, w_gate, w_up, w_down)
    received = swap(send)
    width = 2 * half
    attn_out = jax.ShapeDtypeStruct((a32.shape[0] * LANE // width, width), BF16)
    keep, attn_out = pl.pallas_call(
        keep_kernel,
        in_specs=[vmem_spec()] * 3,
        out_specs=[vmem_spec(), pl.BlockSpec(memory_space=pltpu.HBM)],
        out_shape=[chunked, attn_out],
        scratch_shapes=[
            wide,
            pltpu.VMEM(attn_out.shape, BF16),
            pltpu.SemaphoreType.DMA(()),
        ],
        compiler_params=params,
        cost_estimate=estimate(2 * arrived * half * hidden, 2 * half * hidden),
    )(act, w_down, a32)
    return (attn_out, (keep.astype(F32) + received.astype(F32)).astype(BF16))


def combine_kernel(cap, weight_ref, back_ref, mixed_ref, out_ref, total32):
    rows, width = out_ref.shape
    total = width // LANE
    half = total // 2
    slots = weight_ref.shape[0] // rows
    for c in range(2):
        acc = [
            mixed_ref[r * total + c * half : r * total + (c + 1) * half, :] for r in range(rows)
        ]
        for slot in range(slots):
            e, s = divmod(slot, cap)
            block = back_ref[2 * e + c, s * half : (s + 1) * half, :].astype(F32)
            for r in range(rows):
                acc[r] = acc[r] + weight_ref[r * slots + slot : r * slots + slot + 1, :] * block
        for r in range(rows):
            total32[r * total + c * half : r * total + (c + 1) * half, :] = acc[r]
    for t in range(total):
        out_ref[:, t * LANE : (t + 1) * LANE] = total32[pl.ds(t, rows, stride=total), :].astype(
            BF16
        )


def combine(weights, back, mixed, rows, width, cap):
    return pl.pallas_call(
        functools.partial(combine_kernel, cap),
        in_specs=[vmem_spec()] * 3,
        out_specs=vmem_spec(),
        out_shape=jax.ShapeDtypeStruct((rows, width), BF16),
        scratch_shapes=[pltpu.VMEM(mixed.shape, F32)],
        compiler_params=pltpu.CompilerParams(vmem_limit_bytes=6 << 20),
    )(weights, back, mixed)


def body(
    hidden_in,
    queries,
    new_kv,
    kv_cache,
    lengths,
    w_out,
    w_gate,
    w_up,
    w_down,
    mlp_gain,
    expert_ids,
    route_weight,
):
    devices = lax.axis_size("node")
    rows, width = hidden_in.shape
    expert_count = devices // 2
    cap = max(2, -(-rows * expert_ids.shape[1] // expert_count))
    pairs = [(i, i ^ 1) for i in range(devices)]

    def swap(array):
        return lax.ppermute(array, "node", pairs)

    def exchange(array):
        return lax.all_to_all(array, "node", split_axis=0, concat_axis=0, tiled=True)

    side = devices // 2
    sides = [list(range(side)), list(range(side, devices))]

    def exchange_inside(array):
        return lax.all_to_all(
            array, "node", split_axis=0, concat_axis=0, tiled=True, axis_index_groups=sides
        )

    gain = mlp_gain.reshape(width // LANE, LANE)
    context, weights, pick, h32, gain, w_keep = attention(
        queries,
        new_kv,
        kv_cache,
        lengths,
        expert_ids,
        route_weight,
        hidden_in,
        gain,
        w_out,
        devices,
        cap,
    )
    w_peer = swap(w_out)
    gathered = exchange(context)
    sums = exchange_inside(project(gathered, w_keep, w_peer))
    part, pay = share(sums, h32, pick, expert_count // 2 * cap)
    pay = lax.ppermute(pay, "node", [(i, i ^ side) for i in range(devices)])
    a32, mixed, outgoing = norm_dispatch(part, pay, h32, gain, pick, w_down, devices, cap)
    arrived = exchange_inside(outgoing)
    arrived = arrived.reshape(side, -1, LANE)
    attn_out, paired = experts(arrived, swap, w_gate, w_up, w_down, a32, cap)
    layer_out = combine(weights, exchange(paired), mixed, rows, width, cap)
    return (attn_out, layer_out)


def solution(mesh):
    rows = P(("groups", "node"), None)
    return jax.shard_map(
        body,
        mesh=mesh,
        in_specs=(
            rows,
            rows,
            P(("groups", "node"), None, None),
            P(("groups", "node"), None, None, None),
            P(("groups", "node")),
            P("node", None),
            P("node", None, None),
            P("node", None, None),
            P("node", None, None),
            P(),
            rows,
            rows,
        ),
        out_specs=(rows, rows),
        check_vma=False,
    )
```

```python
import functools
import math

import jax
import jax.numpy as jnp
from jax import lax
from jax.experimental import pallas as pl
from jax.experimental.pallas import tpu as pltpu
from jax.sharding import PartitionSpec as P

HEAD = 128
LANE = 128
F32 = jnp.float32
BF16 = jnp.bfloat16


def vmem_spec():
    return pl.BlockSpec(memory_space=pltpu.VMEM)


def attention_kernel(
    cap,
    q_hbm,
    new_hbm,
    kv_hbm,
    len_hbm,
    ids_hbm,
    route_hbm,
    hidden_hbm,
    gain_hbm,
    w_hbm,
    out_ref,
    weight_ref,
    pick_ref,
    h32_ref,
    gain_ref,
    keep_ref,
    qv,
    nv,
    kv,
    hv,
    lens,
    ids,
    route,
    q32,
    ctx,
    count,
    sems,
):
    rows, heads, _ = ctx.shape
    slots = weight_ref.shape[0] // rows
    cache_len = kv.shape[2]
    kv_heads = kv.shape[3] // HEAD
    group = heads // kv_heads
    core = lax.axis_index("node") % 2
    half = w_hbm.shape[1] // 2
    mine = pl.ds(pl.multiple_of(core * half, half), half)
    pairs = [(ids_hbm, ids), (len_hbm, lens), (q_hbm, qv), (new_hbm, nv)]
    pairs += [(kv_hbm.at[r, i], kv.at[r, i]) for i in range(2) for r in range(rows)]
    pairs += [(hidden_hbm, hv), (gain_hbm, gain_ref), (route_hbm, route)]
    pairs += [(w_hbm.at[:, mine], keep_ref)]
    copies = [
        pltpu.make_async_copy(source, target, sems.at[i])
        for i, (source, target) in enumerate(pairs)
    ]
    for copy in copies:
        copy.start()
    copies[2].wait()
    for h in range(heads):
        q32[pl.ds(h, rows, stride=heads), :] = qv[:, h * HEAD : (h + 1) * HEAD].astype(F32)
    weight_ref[...] = jnp.zeros(weight_ref.shape, F32)
    pick_ref[...] = jnp.zeros(pick_ref.shape, F32)
    for e in range(slots // cap):
        count[e] = 0
    copies[0].wait()
    copies[6 + 2 * rows].wait()
    for row in range(rows):
        for k in range(ids.shape[1]):
            expert = ids[row, k]
            used = count[expert]
            count[expert] = used + 1
            slot = expert * cap + used
            weight_ref[pl.ds(row * slots + slot, 1), :] = jnp.full((1, LANE), route[row, k], F32)
            pick_ref[pl.ds(slot * rows + row, 1), :] = jnp.ones((1, LANE), F32)
    copies[1].wait()
    copies[3].wait()

    scale = 1.0 / math.sqrt(HEAD)
    spot = lax.broadcasted_iota(jnp.int32, (heads, cache_len), 1)
    batch = rows
    for start in range(0, rows, batch):
        chosen = range(start, start + batch)
        for r in chosen:
            copies[4 + r].wait()
        old, new, value, fresh = [], [], [], []
        for r in chosen:
            query = q32[r * heads : (r + 1) * heads, :]
            parts, fresh_key, fresh_value = [], [], []
            for g in range(kv_heads):
                cols = slice(g * HEAD, (g + 1) * HEAD)
                parts.append(
                    lax.dot_general(
                        query[g * group : (g + 1) * group].astype(BF16),
                        kv[r, 0, :, cols],
                        (((1,), (1,)), ((), ())),
                        preferred_element_type=F32,
                    )
                )
                fresh_key.append(jnp.broadcast_to(nv[r, 0:1, cols].astype(F32), (group, HEAD)))
                fresh_value.append(jnp.broadcast_to(nv[r, 1:2, cols].astype(F32), (group, HEAD)))
            scores = jnp.concatenate(parts, axis=0) * scale
            old.append(jnp.where(spot < lens[r], scores, -jnp.inf))
            new.append(
                jnp.sum(query * jnp.concatenate(fresh_key, axis=0), axis=1, keepdims=True) * scale
            )
            fresh.append(jnp.concatenate(fresh_value, axis=0))
        old = jnp.concatenate(old, axis=0)
        new = jnp.concatenate(new, axis=0)
        top = jnp.maximum(jnp.max(old, axis=1, keepdims=True), new)
        old = jnp.exp(old - top)
        new = jnp.exp(new - top)
        share = 1.0 / (jnp.sum(old, axis=1, keepdims=True) + new)
        probs = (old * share).astype(BF16)
        new = (new * share).astype(BF16).astype(F32)
        for r in chosen:
            copies[4 + rows + r].wait()
        for i, r in enumerate(chosen):
            for g in range(kv_heads):
                first = i * heads + g * group
                value.append(
                    jnp.dot(
                        probs[first : first + group],
                        kv[r, 1, :, g * HEAD : (g + 1) * HEAD],
                        preferred_element_type=F32,
                    )
                )
        result = jnp.concatenate(value, axis=0) + new * jnp.concatenate(fresh, axis=0)
        for i, r in enumerate(chosen):
            ctx[r] = result[i * heads : (i + 1) * heads]

    chips = out_ref.shape[0] // 2
    each = heads // chips
    for i in range(chips):
        block = jnp.concatenate(
            [ctx[r, i * each : (i + 1) * each, :] for r in range(rows)], axis=0
        ).astype(BF16)
        out_ref[2 * i] = block
        out_ref[2 * i + 1] = block
    copies[4 + 2 * rows].wait()
    total = h32_ref.shape[0] // rows
    for t in range(total):
        cols = slice(t * LANE, (t + 1) * LANE)
        h32_ref[pl.ds(t, rows, stride=total), :] = hv[:, cols].astype(F32)
    copies[5 + 2 * rows].wait()
    for copy in copies[7 + 2 * rows :]:
        copy.wait()


def attention(
    queries, new_kv, kv_cache, lengths, expert_ids, route_weight, hidden_in, gain, w_out, devices, cap
):
    rows, width = hidden_in.shape
    heads = queries.shape[1] // HEAD
    each = heads // (devices // 2)
    experts = devices // 2
    half = jax.ShapeDtypeStruct((w_out.shape[0], width // 2), BF16)
    table = jax.ShapeDtypeStruct((rows * experts * cap, LANE), F32)
    arrays = (
        queries,
        new_kv,
        kv_cache,
        lengths,
        expert_ids,
        route_weight,
        hidden_in,
        gain,
        w_out,
    )
    return pl.pallas_call(
        functools.partial(attention_kernel, cap),
        in_specs=[pl.BlockSpec(memory_space=pltpu.HBM)] * len(arrays),
        out_specs=[vmem_spec()] * 6,
        out_shape=[
            jax.ShapeDtypeStruct((devices, rows * each, LANE), BF16),
            table,
            table,
            jax.ShapeDtypeStruct((rows * width // LANE, LANE), F32),
            jax.ShapeDtypeStruct(gain.shape, F32),
            half,
        ],
        scratch_shapes=[
            pltpu.VMEM(queries.shape, BF16),
            pltpu.VMEM(new_kv.shape, BF16),
            pltpu.VMEM(kv_cache.shape, BF16),
            pltpu.VMEM(hidden_in.shape, BF16),
            pltpu.SMEM(lengths.shape, jnp.int32),
            pltpu.SMEM(expert_ids.shape, jnp.int32),
            pltpu.SMEM(route_weight.shape, F32),
            pltpu.VMEM((rows * heads, LANE), F32),
            pltpu.VMEM((rows, heads, LANE), F32),
            pltpu.SMEM((experts,), jnp.int32),
            pltpu.SemaphoreType.DMA((8 + 2 * rows,)),
        ],
        compiler_params=pltpu.CompilerParams(vmem_limit_bytes=12 << 20),
    )(*(pltpu.with_memory_space_constraint(array, pltpu.HBM) for array in arrays))


def project_kernel(ctx_ref, own_ref, peer_ref, out_ref, x32, o32):
    devices, per, _ = ctx_ref.shape
    x32[...] = ctx_ref[...].reshape(devices * per, LANE).astype(F32)
    core = lax.axis_index("node") % 2
    held, width = own_ref.shape
    each = 2 * held // LANE
    chunks = width // LANE
    sums = o32.shape[0] // chunks

    def left(first):
        return jnp.concatenate(
            [
                x32[pl.ds(first + j, sums, stride=each), :].astype(BF16)
                for j in range(held // LANE)
            ],
            axis=1,
        )

    def half_cols(first, step):
        return pl.ds(pl.multiple_of(core * width + first, LANE), step)

    own_left = left(core * (held // LANE))
    peer_left = left((1 - core) * (held // LANE))
    step = 512
    for first in range(0, width, step):
        cols = slice(first, first + step)
        total = jnp.dot(own_left, own_ref[:, cols], preferred_element_type=F32) + jnp.dot(
            peer_left, peer_ref[:, half_cols(first, step)], preferred_element_type=F32
        )
        for t in range(step // LANE):
            o32[pl.ds(first // LANE + t, sums, stride=chunks), :] = total[
                :, t * LANE : (t + 1) * LANE
            ]
    sides = o32[...].reshape(2, devices // 2, o32.shape[0] // devices, LANE).astype(BF16)
    for side in range(2):
        out_ref[:, side] = sides[side]


def project(gathered, w_own, w_peer):
    devices, per, _ = gathered.shape
    held, width = w_own.shape
    rows = per // (2 * held // LANE)
    chunks = width // LANE
    return pl.pallas_call(
        project_kernel,
        in_specs=[vmem_spec()] * 3,
        out_specs=vmem_spec(),
        out_shape=jax.ShapeDtypeStruct((devices // 2, 2, rows * chunks, LANE), BF16),
        scratch_shapes=[
            pltpu.VMEM((devices * per, LANE), F32),
            pltpu.VMEM((devices * rows * chunks, LANE), F32),
        ],
        compiler_params=pltpu.CompilerParams(vmem_limit_bytes=12 << 20),
    )(gathered, w_own, w_peer)


def my_side():
    return lax.axis_index("node") // (lax.axis_size("node") // 2)


def share_kernel(sums_ref, h32_ref, pick_ref, part_ref, pay_ref):
    devices, _, per, _ = sums_ref.shape
    size = h32_ref.shape[0]
    rows = pick_ref.shape[0] // (pay_ref.shape[0] - 2 * size) // 2
    total = size // rows
    half = total // 2
    side = my_side()
    for c in range(2):
        for h in range(2):
            acc = sums_ref[c, h].astype(F32)
            for k in range(1, devices // 2):
                acc = acc + sums_ref[2 * k + c, h].astype(F32)
            for r in range(rows):
                first = r * total + c * half
                part_ref[h, first : first + half, :] = acc[r * half : (r + 1) * half]
    pay_ref[:size] = part_ref[1 - side].astype(BF16)
    pay_ref[size : 2 * size] = (part_ref[side] + h32_ref[...]).astype(BF16)
    slots = pay_ref.shape[0] - 2 * size
    lane = lax.broadcasted_iota(jnp.int32, (slots, LANE), 1)
    tile = jnp.zeros((slots, LANE), F32)
    for r in range(rows):
        chosen = pick_ref[pl.ds((1 - side) * slots * rows + r, slots, stride=rows), :]
        tile = jnp.where(lane // (LANE // rows) == r, chosen, tile)
    pay_ref[2 * size :] = tile.astype(BF16)


def share(sums, h32, pick, slots):
    size = h32.shape[0]
    return pl.pallas_call(
        share_kernel,
        in_specs=[vmem_spec()] * 3,
        out_specs=[vmem_spec()] * 2,
        out_shape=[
            jax.ShapeDtypeStruct((2, size, LANE), F32),
            jax.ShapeDtypeStruct((2 * size + slots, LANE), BF16),
        ],
        compiler_params=pltpu.CompilerParams(vmem_limit_bytes=6 << 20),
    )(sums, h32, pick)


def norm_kernel(
    cap, part_ref, pay_ref, h32_ref, gain_ref, pick_ref, down_ref, attn_ref, mixed_ref, out_ref
):
    total = gain_ref.shape[0]
    size = h32_ref.shape[0]
    rows = size // total
    half = total // 2
    slots = pay_ref.shape[0] - 2 * size
    side = my_side()
    attn = part_ref[side] + pay_ref[:size].astype(F32)
    attn_ref[...] = attn
    own = h32_ref[...] + attn.astype(BF16).astype(F32)
    mixed_ref[...] = own
    mirror = part_ref[1 - side] + pay_ref[size : 2 * size].astype(F32)

    def normed(state):
        result = []
        for r in range(rows):
            mixed = state[r * total : (r + 1) * total]
            square = jnp.sum(jnp.sum(mixed * mixed, axis=0, keepdims=True), axis=1, keepdims=True)
            result.append(mixed * lax.rsqrt(square / width_of(total) + 1e-06) * gain_ref[...])
        return result

    tile = pay_ref[2 * size :].astype(F32)
    lane = lax.broadcasted_iota(jnp.int32, (slots, LANE), 1)
    taken = [
        jnp.max(jnp.where(lane // (LANE // rows) == r, tile, 0.0), axis=1, keepdims=True)
        for r in range(rows)
    ]
    first = side * slots * rows
    kept = [pick_ref[pl.ds(first + r, slots, stride=rows), :] for r in range(rows)]
    for state, picks, where in ((own, kept, side), (mirror, taken, 1 - side)):
        lines = normed(state)
        for slot in range(slots):
            chosen = lines[0] * picks[0][slot : slot + 1, :]
            for r in range(1, rows):
                chosen = chosen + lines[r] * picks[r][slot : slot + 1, :]
            chosen = chosen.astype(BF16)
            e, s = divmod(slot, cap)
            for c in range(2):
                out_ref[2 * e + c, where, s * half : (s + 1) * half, :] = chosen[
                    c * half : (c + 1) * half
                ]


def width_of(chunks):
    return chunks * LANE


def norm_dispatch(part, pay, h32, gain, pick, w_down, devices, cap):
    total = gain.shape[0]
    state = jax.ShapeDtypeStruct(h32.shape, F32)
    return pl.pallas_call(
        functools.partial(norm_kernel, cap),
        in_specs=[vmem_spec()] * 6,
        out_specs=[vmem_spec()] * 3,
        out_shape=[
            state,
            state,
            jax.ShapeDtypeStruct((devices // 2, 2, cap * total // 2, LANE), BF16),
        ],
        compiler_params=pltpu.CompilerParams(vmem_limit_bytes=6 << 20),
    )(part, pay, h32, gain, pick, w_down)


def rows_from_chunks(ref, x32, x16):
    devices, per, _ = ref.shape
    arrived, width = x16.shape
    half = width // LANE
    x32[...] = ref[...].reshape(devices * per, LANE).astype(F32)
    for t in range(half):
        x16[:, t * LANE : (t + 1) * LANE] = x32[pl.ds(t, arrived, stride=half), :].astype(BF16)


def chunks_from_rows(result, x32, ref):
    arrived, width = result.shape
    half = width // LANE
    for t in range(half):
        x32[pl.ds(t, arrived, stride=half), :] = result[:, t * LANE : (t + 1) * LANE]
    devices, per, _ = ref.shape
    blocks = x32[...].reshape(devices // 2, 2, per, LANE).astype(BF16)
    for side in range(2):
        ref[side * (devices // 2) : (side + 1) * (devices // 2)] = blocks[:, side]


def half_of(which, size):
    return pl.ds(pl.multiple_of(which * size, size), size)


def own_kernel(own_ref, gate_ref, up_ref, gate_out, up_out, x32, x16):
    rows_from_chunks(own_ref, x32, x16)
    span = half_of(lax.axis_index("node") % 2, x16.shape[1])
    gate_out[...] = jnp.dot(x16[...], gate_ref[0, span, :], preferred_element_type=F32)
    up_out[...] = jnp.dot(x16[...], up_ref[0, span, :], preferred_element_type=F32)


def peer_kernel(
    peer_ref, gate_in, up_in, gate_ref, up_ref, down_ref, act_ref, send_ref, x32, x16
):
    rows_from_chunks(peer_ref, x32, x16)
    span = half_of(1 - lax.axis_index("node") % 2, x16.shape[1])
    gate = gate_in[...] + jnp.dot(x16[...], gate_ref[0, span, :], preferred_element_type=F32)
    up = up_in[...] + jnp.dot(x16[...], up_ref[0, span, :], preferred_element_type=F32)
    act = (gate / (1.0 + jnp.exp(-gate)) * up).astype(BF16)
    act_ref[...] = act
    result = jnp.dot(act, down_ref[0, :, span], preferred_element_type=F32)
    chunks_from_rows(result, x32, send_ref)


def keep_kernel(act_ref, down_ref, a32_ref, keep_ref, attn_hbm, x32, attn, sem):
    rows, width = attn.shape
    total = width // LANE
    for t in range(total):
        attn[:, t * LANE : (t + 1) * LANE] = a32_ref[pl.ds(t, rows, stride=total), :].astype(BF16)
    copy = pltpu.make_async_copy(attn, attn_hbm, sem)
    copy.start()
    size = down_ref.shape[2] // 2
    span = half_of(lax.axis_index("node") % 2, size)
    result = jnp.dot(act_ref[...], down_ref[0, :, span], preferred_element_type=F32)
    chunks_from_rows(result, x32, keep_ref)
    copy.wait()


def estimate(flops, moved):
    return pl.CostEstimate(flops=flops, bytes_accessed=moved, transcendentals=0)


def experts(own, swap, w_gate, w_up, w_down, a32, cap):
    devices, per, _ = own.shape
    half = per // (2 * cap) * LANE
    arrived = devices * 2 * cap
    hidden = w_gate.shape[2]
    chunked = jax.ShapeDtypeStruct((2 * devices, per // 2, LANE), BF16)
    sums = jax.ShapeDtypeStruct((arrived, hidden), F32)
    wide = pltpu.VMEM((devices * per, LANE), F32)
    narrow = pltpu.VMEM((arrived, half), BF16)
    params = pltpu.CompilerParams(vmem_limit_bytes=8 << 20)
    peer = swap(own)
    gate, up = pl.pallas_call(
        own_kernel,
        in_specs=[vmem_spec()] * 3,
        out_specs=[vmem_spec()] * 2,
        out_shape=[sums, sums],
        scratch_shapes=[wide, narrow],
        compiler_params=params,
        cost_estimate=estimate(4 * arrived * half * hidden, 4 * half * hidden),
    )(own, w_gate, w_up)
    act, send = pl.pallas_call(
        peer_kernel,
        in_specs=[vmem_spec()] * 6,
        out_specs=[vmem_spec()] * 2,
        out_shape=[jax.ShapeDtypeStruct((arrived, hidden), BF16), chunked],
        scratch_shapes=[wide, narrow],
        compiler_params=params,
        cost_estimate=estimate(6 * arrived * half * hidden, 6 * half * hidden),
    )(peer, gate, up, w_gate, w_up, w_down)
    received = swap(send)
    width = 2 * half
    attn_out = jax.ShapeDtypeStruct((a32.shape[0] * LANE // width, width), BF16)
    keep, attn_out = pl.pallas_call(
        keep_kernel,
        in_specs=[vmem_spec()] * 3,
        out_specs=[vmem_spec(), pl.BlockSpec(memory_space=pltpu.HBM)],
        out_shape=[chunked, attn_out],
        scratch_shapes=[
            wide,
            pltpu.VMEM(attn_out.shape, BF16),
            pltpu.SemaphoreType.DMA(()),
        ],
        compiler_params=params,
        cost_estimate=estimate(2 * arrived * half * hidden, 2 * half * hidden),
    )(act, w_down, a32)
    return (attn_out, (keep.astype(F32) + received.astype(F32)).astype(BF16))


def combine_kernel(cap, weight_ref, back_ref, mixed_ref, out_ref, total32):
    rows, width = out_ref.shape
    total = width // LANE
    half = total // 2
    slots = weight_ref.shape[0] // rows
    for c in range(2):
        acc = [
            mixed_ref[r * total + c * half : r * total + (c + 1) * half, :] for r in range(rows)
        ]
        for slot in range(slots):
            e, s = divmod(slot, cap)
            block = back_ref[2 * e + c, s * half : (s + 1) * half, :].astype(F32)
            for r in range(rows):
                acc[r] = acc[r] + weight_ref[r * slots + slot : r * slots + slot + 1, :] * block
        for r in range(rows):
            total32[r * total + c * half : r * total + (c + 1) * half, :] = acc[r]
    for t in range(total):
        out_ref[:, t * LANE : (t + 1) * LANE] = total32[pl.ds(t, rows, stride=total), :].astype(
            BF16
        )


def combine(weights, back, mixed, rows, width, cap):
    return pl.pallas_call(
        functools.partial(combine_kernel, cap),
        in_specs=[vmem_spec()] * 3,
        out_specs=vmem_spec(),
        out_shape=jax.ShapeDtypeStruct((rows, width), BF16),
        scratch_shapes=[pltpu.VMEM(mixed.shape, F32)],
        compiler_params=pltpu.CompilerParams(vmem_limit_bytes=6 << 20),
    )(weights, back, mixed)


def body(
    hidden_in,
    queries,
    new_kv,
    kv_cache,
    lengths,
    w_out,
    w_gate,
    w_up,
    w_down,
    mlp_gain,
    expert_ids,
    route_weight,
):
    devices = lax.axis_size("node")
    rows, width = hidden_in.shape
    expert_count = devices // 2
    cap = max(2, -(-rows * expert_ids.shape[1] // expert_count))
    pairs = [(i, i ^ 1) for i in range(devices)]

    def swap(array):
        return lax.ppermute(array, "node", pairs)

    def exchange(array):
        return lax.all_to_all(array, "node", split_axis=0, concat_axis=0, tiled=True)

    side = devices // 2
    sides = [list(range(side)), list(range(side, devices))]

    def exchange_inside(array):
        return lax.all_to_all(
            array, "node", split_axis=0, concat_axis=0, tiled=True, axis_index_groups=sides
        )

    gain = mlp_gain.reshape(width // LANE, LANE)
    context, weights, pick, h32, gain, w_keep = attention(
        queries,
        new_kv,
        kv_cache,
        lengths,
        expert_ids,
        route_weight,
        hidden_in,
        gain,
        w_out,
        devices,
        cap,
    )
    w_peer = swap(w_out)
    gathered = exchange(context)
    sums = exchange_inside(project(gathered, w_keep, w_peer))
    part, pay = share(sums, h32, pick, expert_count // 2 * cap)
    pay = lax.ppermute(pay, "node", [(i, i ^ side) for i in range(devices)])
    a32, mixed, outgoing = norm_dispatch(part, pay, h32, gain, pick, w_down, devices, cap)
    arrived = exchange_inside(outgoing)
    arrived = arrived.reshape(side, -1, LANE)
    attn_out, paired = experts(arrived, swap, w_gate, w_up, w_down, a32, cap)
    layer_out = combine(weights, exchange(paired), mixed, rows, width, cap)
    return (attn_out, layer_out)


def solution(mesh):
    rows = P(("groups", "node"), None)
    return jax.shard_map(
        body,
        mesh=mesh,
        in_specs=(
            rows,
            rows,
            P(("groups", "node"), None, None),
            P(("groups", "node"), None, None, None),
            P(("groups", "node")),
            P("node", None),
            P("node", None, None),
            P("node", None, None),
            P("node", None, None),
            P(),
            rows,
            rows,
        ),
        out_specs=(rows, rows),
        check_vma=False,
    )
```

```python
import functools
import math

import jax
import jax.numpy as jnp
from jax import lax
from jax.experimental import pallas as pl
from jax.experimental.pallas import tpu as pltpu
from jax.sharding import PartitionSpec as P

HEAD = 128
LANE = 128
F32 = jnp.float32
BF16 = jnp.bfloat16


def vmem_spec():
    return pl.BlockSpec(memory_space=pltpu.VMEM)


def attention_kernel(
    cap,
    q_hbm,
    new_hbm,
    kv_hbm,
    len_hbm,
    ids_hbm,
    route_hbm,
    hidden_hbm,
    gain_hbm,
    w_hbm,
    out_ref,
    weight_ref,
    pick_ref,
    h32_ref,
    gain_ref,
    keep_ref,
    qv,
    nv,
    kv,
    hv,
    lens,
    ids,
    route,
    q32,
    ctx,
    count,
    sems,
):
    rows, heads, _ = ctx.shape
    slots = weight_ref.shape[0] // rows
    cache_len = kv.shape[2]
    kv_heads = kv.shape[3] // HEAD
    group = heads // kv_heads
    core = lax.axis_index("node") % 2
    half = w_hbm.shape[1] // 2
    mine = pl.ds(pl.multiple_of(core * half, half), half)
    pairs = [(ids_hbm, ids), (len_hbm, lens), (q_hbm, qv), (new_hbm, nv)]
    pairs += [(kv_hbm.at[r, i], kv.at[r, i]) for i in range(2) for r in range(rows)]
    pairs += [(hidden_hbm, hv), (gain_hbm, gain_ref), (route_hbm, route)]
    pairs += [(w_hbm.at[:, mine], keep_ref)]
    copies = [
        pltpu.make_async_copy(source, target, sems.at[i])
        for i, (source, target) in enumerate(pairs)
    ]
    for copy in copies[2:3] + copies[:1] + copies[4 : 4 + rows] + copies[1:2] + copies[3:4]:
        copy.start()
    for copy in copies[4 + 2 * rows : 7 + 2 * rows] + copies[4 + rows : 4 + 2 * rows]:
        copy.start()
    copies[7 + 2 * rows].start()
    copies[2].wait()
    for h in range(heads):
        q32[pl.ds(h, rows, stride=heads), :] = qv[:, h * HEAD : (h + 1) * HEAD].astype(F32)
    weight_ref[...] = jnp.zeros(weight_ref.shape, F32)
    pick_ref[...] = jnp.zeros(pick_ref.shape, F32)
    for e in range(slots // cap):
        count[e] = 0
    copies[0].wait()
    copies[6 + 2 * rows].wait()
    for row in range(rows):
        for k in range(ids.shape[1]):
            expert = ids[row, k]
            used = count[expert]
            count[expert] = used + 1
            slot = expert * cap + used
            weight_ref[pl.ds(row * slots + slot, 1), :] = jnp.full((1, LANE), route[row, k], F32)
            pick_ref[pl.ds(slot * rows + row, 1), :] = jnp.ones((1, LANE), F32)
    copies[4 + 2 * rows].wait()
    total = h32_ref.shape[0] // rows
    for t in range(total):
        cols = slice(t * LANE, (t + 1) * LANE)
        h32_ref[pl.ds(t, rows, stride=total), :] = hv[:, cols].astype(F32)
    copies[1].wait()
    copies[3].wait()

    scale = 1.0 / math.sqrt(HEAD)
    spot = lax.broadcasted_iota(jnp.int32, (heads, cache_len), 1)
    batch = rows
    for start in range(0, rows, batch):
        chosen = range(start, start + batch)
        for r in chosen:
            copies[4 + r].wait()
        old, new, value, fresh = [], [], [], []
        for r in chosen:
            query = q32[r * heads : (r + 1) * heads, :]
            parts, fresh_key, fresh_value = [], [], []
            for g in range(kv_heads):
                cols = slice(g * HEAD, (g + 1) * HEAD)
                parts.append(
                    lax.dot_general(
                        query[g * group : (g + 1) * group].astype(BF16),
                        kv[r, 0, :, cols],
                        (((1,), (1,)), ((), ())),
                        preferred_element_type=F32,
                    )
                )
                fresh_key.append(jnp.broadcast_to(nv[r, 0:1, cols].astype(F32), (group, HEAD)))
                fresh_value.append(jnp.broadcast_to(nv[r, 1:2, cols].astype(F32), (group, HEAD)))
            scores = jnp.concatenate(parts, axis=0) * scale
            old.append(jnp.where(spot < lens[r], scores, -jnp.inf))
            new.append(
                jnp.sum(query * jnp.concatenate(fresh_key, axis=0), axis=1, keepdims=True) * scale
            )
            fresh.append(jnp.concatenate(fresh_value, axis=0))
        old = jnp.concatenate(old, axis=0)
        new = jnp.concatenate(new, axis=0)
        top = jnp.maximum(jnp.max(old, axis=1, keepdims=True), new)
        old = jnp.exp(old - top)
        new = jnp.exp(new - top)
        share = 1.0 / (jnp.sum(old, axis=1, keepdims=True) + new)
        probs = (old * share).astype(BF16)
        new = (new * share).astype(BF16).astype(F32)
        for r in chosen:
            copies[4 + rows + r].wait()
        for i, r in enumerate(chosen):
            for g in range(kv_heads):
                first = i * heads + g * group
                value.append(
                    jnp.dot(
                        probs[first : first + group],
                        kv[r, 1, :, g * HEAD : (g + 1) * HEAD],
                        preferred_element_type=F32,
                    )
                )
        result = jnp.concatenate(value, axis=0) + new * jnp.concatenate(fresh, axis=0)
        for i, r in enumerate(chosen):
            ctx[r] = result[i * heads : (i + 1) * heads]

    chips = out_ref.shape[0] // 2
    each = heads // chips
    for i in range(chips):
        block = jnp.concatenate(
            [ctx[r, i * each : (i + 1) * each, :] for r in range(rows)], axis=0
        ).astype(BF16)
        out_ref[2 * i] = block
        out_ref[2 * i + 1] = block
    copies[5 + 2 * rows].wait()
    for copy in copies[7 + 2 * rows :]:
        copy.wait()


def attention(
    queries, new_kv, kv_cache, lengths, expert_ids, route_weight, hidden_in, gain, w_out, devices, cap
):
    rows, width = hidden_in.shape
    heads = queries.shape[1] // HEAD
    each = heads // (devices // 2)
    experts = devices // 2
    half = jax.ShapeDtypeStruct((w_out.shape[0], width // 2), BF16)
    table = jax.ShapeDtypeStruct((rows * experts * cap, LANE), F32)
    arrays = (
        queries,
        new_kv,
        kv_cache,
        lengths,
        expert_ids,
        route_weight,
        hidden_in,
        gain,
        w_out,
    )
    return pl.pallas_call(
        functools.partial(attention_kernel, cap),
        in_specs=[pl.BlockSpec(memory_space=pltpu.HBM)] * len(arrays),
        out_specs=[vmem_spec()] * 6,
        out_shape=[
            jax.ShapeDtypeStruct((devices, rows * each, LANE), BF16),
            table,
            table,
            jax.ShapeDtypeStruct((rows * width // LANE, LANE), F32),
            jax.ShapeDtypeStruct(gain.shape, F32),
            half,
        ],
        scratch_shapes=[
            pltpu.VMEM(queries.shape, BF16),
            pltpu.VMEM(new_kv.shape, BF16),
            pltpu.VMEM(kv_cache.shape, BF16),
            pltpu.VMEM(hidden_in.shape, BF16),
            pltpu.SMEM(lengths.shape, jnp.int32),
            pltpu.SMEM(expert_ids.shape, jnp.int32),
            pltpu.SMEM(route_weight.shape, F32),
            pltpu.VMEM((rows * heads, LANE), F32),
            pltpu.VMEM((rows, heads, LANE), F32),
            pltpu.SMEM((experts,), jnp.int32),
            pltpu.SemaphoreType.DMA((8 + 2 * rows,)),
        ],
        compiler_params=pltpu.CompilerParams(vmem_limit_bytes=12 << 20),
    )(*(pltpu.with_memory_space_constraint(array, pltpu.HBM) for array in arrays))


def project_kernel(ctx_ref, own_ref, peer_ref, out_ref, x32, o32):
    devices, per, _ = ctx_ref.shape
    x32[...] = ctx_ref[...].reshape(devices * per, LANE).astype(F32)
    core = lax.axis_index("node") % 2
    held, width = own_ref.shape
    each = 2 * held // LANE
    chunks = width // LANE
    sums = o32.shape[0] // chunks

    def left(first):
        return jnp.concatenate(
            [
                x32[pl.ds(first + j, sums, stride=each), :].astype(BF16)
                for j in range(held // LANE)
            ],
            axis=1,
        )

    def half_cols(first, step):
        return pl.ds(pl.multiple_of(core * width + first, LANE), step)

    own_left = left(core * (held // LANE))
    peer_left = left((1 - core) * (held // LANE))
    step = 512
    for first in range(0, width, step):
        cols = slice(first, first + step)
        total = jnp.dot(own_left, own_ref[:, cols], preferred_element_type=F32) + jnp.dot(
            peer_left, peer_ref[:, half_cols(first, step)], preferred_element_type=F32
        )
        for t in range(step // LANE):
            o32[pl.ds(first // LANE + t, sums, stride=chunks), :] = total[
                :, t * LANE : (t + 1) * LANE
            ]
    sides = o32[...].reshape(2, devices // 2, o32.shape[0] // devices, LANE).astype(BF16)
    for side in range(2):
        out_ref[:, side] = sides[side]


def project(gathered, w_own, w_peer):
    devices, per, _ = gathered.shape
    held, width = w_own.shape
    rows = per // (2 * held // LANE)
    chunks = width // LANE
    return pl.pallas_call(
        project_kernel,
        in_specs=[vmem_spec()] * 3,
        out_specs=vmem_spec(),
        out_shape=jax.ShapeDtypeStruct((devices // 2, 2, rows * chunks, LANE), BF16),
        scratch_shapes=[
            pltpu.VMEM((devices * per, LANE), F32),
            pltpu.VMEM((devices * rows * chunks, LANE), F32),
        ],
        compiler_params=pltpu.CompilerParams(vmem_limit_bytes=12 << 20),
    )(gathered, w_own, w_peer)


def my_side():
    return lax.axis_index("node") // (lax.axis_size("node") // 2)


def share_kernel(sums_ref, h32_ref, pick_ref, part_ref, pay_ref):
    devices, _, per, _ = sums_ref.shape
    size = h32_ref.shape[0]
    rows = pick_ref.shape[0] // (pay_ref.shape[0] - 2 * size) // 2
    total = size // rows
    half = total // 2
    side = my_side()
    for c in range(2):
        for h in range(2):
            acc = sums_ref[c, h].astype(F32)
            for k in range(1, devices // 2):
                acc = acc + sums_ref[2 * k + c, h].astype(F32)
            for r in range(rows):
                first = r * total + c * half
                part_ref[h, first : first + half, :] = acc[r * half : (r + 1) * half]
    pay_ref[:size] = part_ref[1 - side].astype(BF16)
    pay_ref[size : 2 * size] = (part_ref[side] + h32_ref[...]).astype(BF16)
    slots = pay_ref.shape[0] - 2 * size
    lane = lax.broadcasted_iota(jnp.int32, (slots, LANE), 1)
    tile = jnp.zeros((slots, LANE), F32)
    for r in range(rows):
        chosen = pick_ref[pl.ds((1 - side) * slots * rows + r, slots, stride=rows), :]
        tile = jnp.where(lane // (LANE // rows) == r, chosen, tile)
    pay_ref[2 * size :] = tile.astype(BF16)


def share(sums, h32, pick, slots):
    size = h32.shape[0]
    return pl.pallas_call(
        share_kernel,
        in_specs=[vmem_spec()] * 3,
        out_specs=[vmem_spec()] * 2,
        out_shape=[
            jax.ShapeDtypeStruct((2, size, LANE), F32),
            jax.ShapeDtypeStruct((2 * size + slots, LANE), BF16),
        ],
        compiler_params=pltpu.CompilerParams(vmem_limit_bytes=6 << 20),
    )(sums, h32, pick)


def norm_kernel(
    cap, part_ref, pay_ref, h32_ref, gain_ref, pick_ref, down_ref, attn_ref, mixed_ref, out_ref
):
    total = gain_ref.shape[0]
    size = h32_ref.shape[0]
    rows = size // total
    half = total // 2
    slots = pay_ref.shape[0] - 2 * size
    side = my_side()
    attn = part_ref[side] + pay_ref[:size].astype(F32)
    attn_ref[...] = attn
    own = h32_ref[...] + attn.astype(BF16).astype(F32)
    mixed_ref[...] = own
    mirror = part_ref[1 - side] + pay_ref[size : 2 * size].astype(F32)

    def normed(state):
        result = []
        for r in range(rows):
            mixed = state[r * total : (r + 1) * total]
            square = jnp.sum(jnp.sum(mixed * mixed, axis=0, keepdims=True), axis=1, keepdims=True)
            result.append(mixed * lax.rsqrt(square / width_of(total) + 1e-06) * gain_ref[...])
        return result

    tile = pay_ref[2 * size :].astype(F32)
    lane = lax.broadcasted_iota(jnp.int32, (slots, LANE), 1)
    taken = [
        jnp.max(jnp.where(lane // (LANE // rows) == r, tile, 0.0), axis=1, keepdims=True)
        for r in range(rows)
    ]
    first = side * slots * rows
    kept = [pick_ref[pl.ds(first + r, slots, stride=rows), :] for r in range(rows)]
    for state, picks, where in ((own, kept, side), (mirror, taken, 1 - side)):
        lines = normed(state)
        for slot in range(slots):
            chosen = lines[0] * picks[0][slot : slot + 1, :]
            for r in range(1, rows):
                chosen = chosen + lines[r] * picks[r][slot : slot + 1, :]
            chosen = chosen.astype(BF16)
            e, s = divmod(slot, cap)
            for c in range(2):
                out_ref[2 * e + c, where, s * half : (s + 1) * half, :] = chosen[
                    c * half : (c + 1) * half
                ]


def width_of(chunks):
    return chunks * LANE


def norm_dispatch(part, pay, h32, gain, pick, w_down, devices, cap):
    total = gain.shape[0]
    state = jax.ShapeDtypeStruct(h32.shape, F32)
    return pl.pallas_call(
        functools.partial(norm_kernel, cap),
        in_specs=[vmem_spec()] * 6,
        out_specs=[vmem_spec()] * 3,
        out_shape=[
            state,
            state,
            jax.ShapeDtypeStruct((devices // 2, 2, cap * total // 2, LANE), BF16),
        ],
        compiler_params=pltpu.CompilerParams(vmem_limit_bytes=6 << 20),
    )(part, pay, h32, gain, pick, w_down)


def rows_from_chunks(ref, x32, x16):
    devices, per, _ = ref.shape
    arrived, width = x16.shape
    half = width // LANE
    x32[...] = ref[...].reshape(devices * per, LANE).astype(F32)
    for t in range(half):
        x16[:, t * LANE : (t + 1) * LANE] = x32[pl.ds(t, arrived, stride=half), :].astype(BF16)


def chunks_from_rows(result, x32, ref):
    arrived, width = result.shape
    half = width // LANE
    for t in range(half):
        x32[pl.ds(t, arrived, stride=half), :] = result[:, t * LANE : (t + 1) * LANE]
    devices, per, _ = ref.shape
    blocks = x32[...].reshape(devices // 2, 2, per, LANE).astype(BF16)
    for side in range(2):
        ref[side * (devices // 2) : (side + 1) * (devices // 2)] = blocks[:, side]


def half_of(which, size):
    return pl.ds(pl.multiple_of(which * size, size), size)


def own_kernel(own_ref, gate_ref, up_ref, gate_out, up_out, x32, x16):
    rows_from_chunks(own_ref, x32, x16)
    span = half_of(lax.axis_index("node") % 2, x16.shape[1])
    gate_out[...] = jnp.dot(x16[...], gate_ref[0, span, :], preferred_element_type=F32)
    up_out[...] = jnp.dot(x16[...], up_ref[0, span, :], preferred_element_type=F32)


def peer_kernel(
    peer_ref, gate_in, up_in, gate_ref, up_ref, down_ref, act_ref, send_ref, x32, x16
):
    rows_from_chunks(peer_ref, x32, x16)
    span = half_of(1 - lax.axis_index("node") % 2, x16.shape[1])
    gate = gate_in[...] + jnp.dot(x16[...], gate_ref[0, span, :], preferred_element_type=F32)
    up = up_in[...] + jnp.dot(x16[...], up_ref[0, span, :], preferred_element_type=F32)
    act = (gate / (1.0 + jnp.exp(-gate)) * up).astype(BF16)
    act_ref[...] = act
    result = jnp.dot(act, down_ref[0, :, span], preferred_element_type=F32)
    chunks_from_rows(result, x32, send_ref)


def keep_kernel(act_ref, down_ref, a32_ref, keep_ref, attn_hbm, x32, attn, sem):
    rows, width = attn.shape
    total = width // LANE
    for t in range(total):
        attn[:, t * LANE : (t + 1) * LANE] = a32_ref[pl.ds(t, rows, stride=total), :].astype(BF16)
    copy = pltpu.make_async_copy(attn, attn_hbm, sem)
    copy.start()
    size = down_ref.shape[2] // 2
    span = half_of(lax.axis_index("node") % 2, size)
    result = jnp.dot(act_ref[...], down_ref[0, :, span], preferred_element_type=F32)
    chunks_from_rows(result, x32, keep_ref)
    copy.wait()


def estimate(flops, moved):
    return pl.CostEstimate(flops=flops, bytes_accessed=moved, transcendentals=0)


def experts(own, swap, w_gate, w_up, w_down, a32, cap):
    devices, per, _ = own.shape
    half = per // (2 * cap) * LANE
    arrived = devices * 2 * cap
    hidden = w_gate.shape[2]
    chunked = jax.ShapeDtypeStruct((2 * devices, per // 2, LANE), BF16)
    sums = jax.ShapeDtypeStruct((arrived, hidden), F32)
    wide = pltpu.VMEM((devices * per, LANE), F32)
    narrow = pltpu.VMEM((arrived, half), BF16)
    params = pltpu.CompilerParams(vmem_limit_bytes=8 << 20)
    peer = swap(own)
    gate, up = pl.pallas_call(
        own_kernel,
        in_specs=[vmem_spec()] * 3,
        out_specs=[vmem_spec()] * 2,
        out_shape=[sums, sums],
        scratch_shapes=[wide, narrow],
        compiler_params=params,
        cost_estimate=estimate(4 * arrived * half * hidden, 4 * half * hidden),
    )(own, w_gate, w_up)
    act, send = pl.pallas_call(
        peer_kernel,
        in_specs=[vmem_spec()] * 6,
        out_specs=[vmem_spec()] * 2,
        out_shape=[jax.ShapeDtypeStruct((arrived, hidden), BF16), chunked],
        scratch_shapes=[wide, narrow],
        compiler_params=params,
        cost_estimate=estimate(6 * arrived * half * hidden, 6 * half * hidden),
    )(peer, gate, up, w_gate, w_up, w_down)
    received = swap(send)
    width = 2 * half
    attn_out = jax.ShapeDtypeStruct((a32.shape[0] * LANE // width, width), BF16)
    keep, attn_out = pl.pallas_call(
        keep_kernel,
        in_specs=[vmem_spec()] * 3,
        out_specs=[vmem_spec(), pl.BlockSpec(memory_space=pltpu.HBM)],
        out_shape=[chunked, attn_out],
        scratch_shapes=[
            wide,
            pltpu.VMEM(attn_out.shape, BF16),
            pltpu.SemaphoreType.DMA(()),
        ],
        compiler_params=params,
        cost_estimate=estimate(2 * arrived * half * hidden, 2 * half * hidden),
    )(act, w_down, a32)
    return (attn_out, (keep.astype(F32) + received.astype(F32)).astype(BF16))


def combine_kernel(cap, weight_ref, back_ref, mixed_ref, out_ref, total32):
    rows, width = out_ref.shape
    total = width // LANE
    half = total // 2
    slots = weight_ref.shape[0] // rows
    for c in range(2):
        acc = [
            mixed_ref[r * total + c * half : r * total + (c + 1) * half, :] for r in range(rows)
        ]
        for slot in range(slots):
            e, s = divmod(slot, cap)
            block = back_ref[2 * e + c, s * half : (s + 1) * half, :].astype(F32)
            for r in range(rows):
                acc[r] = acc[r] + weight_ref[r * slots + slot : r * slots + slot + 1, :] * block
        for r in range(rows):
            total32[r * total + c * half : r * total + (c + 1) * half, :] = acc[r]
    for t in range(total):
        out_ref[:, t * LANE : (t + 1) * LANE] = total32[pl.ds(t, rows, stride=total), :].astype(
            BF16
        )


def combine(weights, back, mixed, rows, width, cap):
    return pl.pallas_call(
        functools.partial(combine_kernel, cap),
        in_specs=[vmem_spec()] * 3,
        out_specs=vmem_spec(),
        out_shape=jax.ShapeDtypeStruct((rows, width), BF16),
        scratch_shapes=[pltpu.VMEM(mixed.shape, F32)],
        compiler_params=pltpu.CompilerParams(vmem_limit_bytes=6 << 20),
    )(weights, back, mixed)


def body(
    hidden_in,
    queries,
    new_kv,
    kv_cache,
    lengths,
    w_out,
    w_gate,
    w_up,
    w_down,
    mlp_gain,
    expert_ids,
    route_weight,
):
    devices = lax.axis_size("node")
    rows, width = hidden_in.shape
    expert_count = devices // 2
    cap = max(2, -(-rows * expert_ids.shape[1] // expert_count))
    pairs = [(i, i ^ 1) for i in range(devices)]

    def swap(array):
        return lax.ppermute(array, "node", pairs)

    def exchange(array):
        return lax.all_to_all(array, "node", split_axis=0, concat_axis=0, tiled=True)

    side = devices // 2
    sides = [list(range(side)), list(range(side, devices))]

    def exchange_inside(array):
        return lax.all_to_all(
            array, "node", split_axis=0, concat_axis=0, tiled=True, axis_index_groups=sides
        )

    gain = mlp_gain.reshape(width // LANE, LANE)
    context, weights, pick, h32, gain, w_keep = attention(
        queries,
        new_kv,
        kv_cache,
        lengths,
        expert_ids,
        route_weight,
        hidden_in,
        gain,
        w_out,
        devices,
        cap,
    )
    w_peer = swap(w_out)
    gathered = exchange(context)
    sums = exchange_inside(project(gathered, w_keep, w_peer))
    part, pay = share(sums, h32, pick, expert_count // 2 * cap)
    pay = lax.ppermute(pay, "node", [(i, i ^ side) for i in range(devices)])
    a32, mixed, outgoing = norm_dispatch(part, pay, h32, gain, pick, w_down, devices, cap)
    arrived = exchange_inside(outgoing)
    arrived = arrived.reshape(side, -1, LANE)
    attn_out, paired = experts(arrived, swap, w_gate, w_up, w_down, a32, cap)
    layer_out = combine(weights, exchange(paired), mixed, rows, width, cap)
    return (attn_out, layer_out)


def solution(mesh):
    rows = P(("groups", "node"), None)
    return jax.shard_map(
        body,
        mesh=mesh,
        in_specs=(
            rows,
            rows,
            P(("groups", "node"), None, None),
            P(("groups", "node"), None, None, None),
            P(("groups", "node")),
            P("node", None),
            P("node", None, None),
            P("node", None, None),
            P("node", None, None),
            P(),
            rows,
            rows,
        ),
        out_specs=(rows, rows),
        check_vma=False,
    )
```
